128 devices in a mesh: gx: 16 (over y, x), gy: 8 (over z, core).
Axes of the slice: x: 4, y: 4, z: 4, core: 2. Of those that a mesh axis runs over, the one named last changes fastest.
Arguments:
- mentions: bfloat16 [16384, 1024], P(('gx', 'gy')), may hold values from -150 to 150
- centroids: bfloat16 [128, 1024], replicated, may hold values from -6 to 6
- clusters: int32 [16384, 9], P(('gx', 'gy')), may hold values from 0 to 127, all different within a row; in each aligned block of 128 rows (0 to 127, 128 to 255, ...) at most 13 rows name the same one
- gold_entity: int32 [16384], P(('gx', 'gy')), may hold values from 0 to 1023
- cluster_map: int32 [128], replicated, may hold values from 0 to 127, each once
- entities: bfloat16 [128, 1024, 1024], P(('gx', 'gy')), may hold values from -6 to 6
- m_state: float32 [128, 1024, 1024], P(('gx', 'gy')), may hold values from -6 to 6
- v_state: float32 [128, 1024, 1024], P(('gx', 'gy')), may hold values from 0.1 to 2
Outputs:
- losses: float32 [16384], P(('gx', 'gy'))
- mention_grad: float32 [16384, 1024], P(('gx', 'gy'))
- centroid_grad: float32 [128, 1024], P(('gx', 'gy'))
- new_entities: bfloat16 [128, 1024, 1024], P(('gx', 'gy'))
- new_m: float32 [128, 1024, 1024], P(('gx', 'gy'))
- new_v: float32 [128, 1024, 1024], P(('gx', 'gy'))
The draws below stay inside these ranges and needn't reach their ends.
Inputs may be any that keep to these rules, and one draw needn't show every extreme that they name: Each row names 9 different clusters, the gold one first. Among the mentions of one device no cluster is named more than 13 times, and in every draw some cluster is named exactly 13 times among the mentions of some device. A permutation: cluster c sits at row cluster_map[c] of entities, m_state and v_state.
All inputs are finite; a program needn't handle non-finite values.
Results may differ from the reference program's by a relative error of at most 0.0027.
Values may be sent and summed in bfloat16 or wider, within the bound.
A program may use at most 128 MiB of HBM per device.

```python
import math
import jax
import jax.numpy as jnp
import numpy as np
from jax import lax

D = 1024
ENTS = 1024
PICKS = 9
M_DEV = 128
CLUSTERS = 128
MENTIONS = 16384
MOST = 13
N_GX = 16
N_GY = 8


def draw_mentions(key, part):
    key = jax.random.fold_in(key, 11)
    first_key = jax.random.fold_in(key, 0)
    base = jax.random.normal(first_key, (MENTIONS, D), jnp.float32)
    return jnp.clip(base, -6.0, 6.0).astype(jnp.bfloat16)


def with_ends(result, own_key, low, top_value):
    spot = [jax.random.randint(jax.random.fold_in(own_key, axis), (), 0, length) for axis, length in enumerate(result.shape)]
    longest = result.shape.index(max(result.shape))
    neighbour = spot[:longest] + [(spot[longest] + 1) % result.shape[longest]] + spot[longest + 1:]
    return result.at[tuple(spot)].set(low).at[tuple(neighbour)].set(top_value)


def levels(own_key, dims, shards, smallest, largest):
    level = 1.0
    for dim, parts in shards:
        heights = jax.random.uniform(jax.random.fold_in(jax.random.fold_in(own_key, 6), dim), (parts,), jnp.float32, smallest / len(shards), largest / len(shards))
        level = level * jnp.repeat(jnp.exp(heights), dims[dim] // parts).reshape((-1,) + (1,) * (len(dims) - 1 - dim))
    return level


def routed_block(stream_key, own, number, rows, count, top, limit, slope):
    ranking = jax.random.permutation(stream_key, count)
    packed, usual = portions_of(count, rows * top, limit, slope, True), portions_of(count, rows * top, limit, slope, False)
    places = jnp.arange(count)

    def named(lengths, offset_by):
        used = int((lengths > 0).sum())
        fixed = max(1, used // 4)
        passed = fixed + (places - fixed + offset_by * (used - fixed)) % max(1, count - fixed)
        return jnp.zeros((count,), jnp.int32).at[ranking[jnp.where(places < fixed, places, passed)]].set(jnp.asarray(lengths, jnp.int32))

    lengths = jnp.where(number % 4 == 0, named(packed, number // 4), named(usual, number - number // 4 - 1))
    mixed = jax.random.permutation(jax.random.fold_in(own, 3), count)
    donor, receiver = mixed[0:count // 2 * 2:2], mixed[1:count // 2 * 2:2]
    slack = jnp.minimum(lengths[donor] - 1, limit - lengths[receiver]) // 2
    slack = jnp.where((donor == ranking[0]) | (receiver == ranking[0]) | (lengths[receiver] == 0), 0, jnp.maximum(slack, 0))
    passed = jax.random.randint(jax.random.fold_in(own, 4), (count // 2,), 0, 1 << 20) % (slack + 1)
    lengths = lengths.at[donor].add(-passed).at[receiver].add(passed)
    items = jnp.searchsorted(jnp.cumsum(lengths), jnp.arange(rows * top), side="right").astype(jnp.int32)
    grid = items.reshape(top, rows).T
    grid = grid[jax.random.permutation(jax.random.fold_in(own, 1), rows)]
    offset_by = jax.random.randint(jax.random.fold_in(own, 2), (rows, 1), 0, top)
    return jnp.take_along_axis(grid, (jnp.arange(top)[None, :] + offset_by) % top, axis=1)


def portions_of(amount, total, limit, skew, full):
    loads = [(1 << 20) // math.isqrt(rank ** skew) + 1 for rank in range(1, amount + 1)]
    largest = limit if full else min(limit, max(-(-total // amount), total * loads[0] // sum(loads)))
    least = 1 if total - largest >= amount - 1 else 0
    given, spare = [largest] + [least] * (amount - 1), total - largest - least * (amount - 1)
    while spare > 0:
        free = [i for i in range(1, amount) if given[i] < largest] or [i for i in range(1, amount) if given[i] < limit]
        pool, budget = sum([loads[i] for i in free]), spare
        for i in free:
            extra = min(limit - given[i], max(1, budget * loads[i] // pool), spare)
            given[i] = given[i] + extra
            spare = spare - extra
    return np.array(given)


def bell_draw(stream_key, extent, spread, reach, cuts=(), kind=jnp.bfloat16):
    result = jax.random.normal(stream_key, extent, jnp.float32) * spread
    if len(cuts) > 0:
        result = levels(stream_key, extent, cuts, -0.22, 0.18) * result
    return jnp.clip(result, min=-reach, max=reach).astype(kind)


def setup_inputs(seed: int = 0) -> dict:
    arg_keys = jax.random.split(jax.random.key(seed), 9)
    mentions = draw_mentions(jax.random.fold_in(arg_keys[8], 71), 0)
    centroids = bell_draw(arg_keys[1], (CLUSTERS, D), 1.0, 6.0)
    clusters_keys = jax.random.split(jax.random.fold_in(arg_keys[2], 1), MENTIONS // M_DEV)
    clusters_turns = jax.random.permutation(jax.random.fold_in(arg_keys[2], 3), MENTIONS // M_DEV)
    clusters = jax.vmap(lambda own, number: routed_block(jax.random.fold_in(arg_keys[2], 2), own, number, M_DEV, CLUSTERS, PICKS, MOST, 2))(clusters_keys, clusters_turns).reshape((MENTIONS, PICKS))
    gold_entity = with_ends(jax.random.randint(arg_keys[3], (MENTIONS,), 0, ENTS), jax.random.fold_in(arg_keys[3], 1), 0, ENTS - 1).astype(jnp.int32)
    cluster_map = jax.random.permutation(arg_keys[4], CLUSTERS).astype(jnp.int32)
    entities = bell_draw(arg_keys[5], (CLUSTERS, ENTS, D), 1.0, 6.0, ((0, 128),))
    m_state = bell_draw(arg_keys[6], (CLUSTERS, ENTS, D), 1.0, 6.0, ((0, 128),), jnp.float32)
    v_state = jnp.clip(jnp.exp(math.log(2.0) - 2.9957323 * jax.random.uniform(arg_keys[7], (CLUSTERS, ENTS, D), jnp.float32) ** levels(arg_keys[7], (CLUSTERS, ENTS, D), ((0, 128),), -0.2, 0.2)), 0.1, 2.0)
    return {"mentions": mentions, "centroids": centroids, "clusters": clusters, "gold_entity": gold_entity, "cluster_map": cluster_map, "entities": entities, "m_state": m_state, "v_state": v_state}


BETA_ONE = 0.9
BETA_TWO = 0.999
STEP_SIZE = 0.05
EPSILON = 1e-08

def block_ranks(slot_ids):
    count = slot_ids.shape[0]
    order = jnp.arange(count, dtype=jnp.int32)
    earlier = (slot_ids[None, :] == slot_ids[:, None]) & (order[None, :] < order[:, None])
    return lax.optimization_barrier(jnp.sum(earlier.astype(jnp.int32), axis=1)).astype(jnp.int32)

def reference(mentions, centroids, clusters, gold_entity, cluster_map, entities, m_state, v_state):
    inverse_root = 1.0 / math.sqrt(D)
    devices = N_GX * N_GY
    cluster_scores = jnp.dot(mentions, centroids.T, preferred_element_type=jnp.float32) * inverse_root
    cluster_norm = jax.nn.logsumexp(cluster_scores, axis=1)
    gold_hot = (jnp.arange(CLUSTERS, dtype=jnp.int32)[None, :] == clusters[:, 0:1]).astype(jnp.float32)
    cluster_gold = lax.optimization_barrier(jnp.sum(cluster_scores * gold_hot, axis=1))
    cluster_coef = (jnp.exp(cluster_scores - cluster_norm[:, None]) - gold_hot).astype(jnp.bfloat16)
    direct_grad = jnp.dot(cluster_coef, centroids, preferred_element_type=jnp.float32) * inverse_root
    centroid_grad = jnp.dot(cluster_coef.T, mentions, preferred_element_type=jnp.float32) * inverse_root
    pair_count = MENTIONS * PICKS
    pair_ids = jnp.arange(pair_count, dtype=jnp.int32)
    slot_ids = jnp.take(cluster_map, clusters.reshape(-1)).astype(jnp.int32)
    ranks = lax.map(block_ranks, slot_ids.reshape(devices, M_DEV * PICKS)).reshape(-1)
    sources = pair_ids // (M_DEV * PICKS)
    table_width = devices * MOST
    places = slot_ids * table_width + sources * MOST + ranks
    table = jnp.full((CLUSTERS * table_width,), -1, jnp.int32).at[places].set(pair_ids)
    table = table.reshape(CLUSTERS, table_width)
    gold_tags = jnp.where(pair_ids % PICKS == 0, gold_entity[pair_ids // PICKS], -1).astype(jnp.int32)

    def gather_rows(row_ids):
        valid = row_ids >= 0
        safe = jnp.where(valid, row_ids, 0)
        rows = jnp.where(valid[:, None], mentions[safe // PICKS], jnp.zeros((), jnp.bfloat16))
        tags = jnp.where(valid, gold_tags[safe], -1)
        hits = (jnp.arange(ENTS, dtype=jnp.int32)[None, :] == tags[:, None]).astype(jnp.float32)
        return (rows, hits, valid, safe)

    def score_slot(items):
        row_ids, table_rows = items
        rows, hits, valid, safe = gather_rows(row_ids)
        scores = jnp.dot(rows, table_rows.T, preferred_element_type=jnp.float32) * inverse_root
        return (jax.nn.logsumexp(scores, axis=1), lax.optimization_barrier(jnp.sum(scores * hits, axis=1)))
    part_norm, part_gold = lax.map(score_slot, (table, entities))
    pair_norm = part_norm.reshape(-1)[places].reshape(MENTIONS, PICKS)
    entity_gold = part_gold.reshape(-1)[places].reshape(MENTIONS, PICKS)[:, 0]
    entity_norm = jax.nn.logsumexp(pair_norm, axis=1)
    losses = cluster_norm - cluster_gold + entity_norm - entity_gold
    totals = jnp.zeros((CLUSTERS * table_width,), jnp.float32).at[places].set(jnp.repeat(entity_norm, PICKS))
    totals = totals.reshape(CLUSTERS, table_width)

    def update(carry, items):
        row_ids, total_rows, table_rows, first, second = items
        rows, hits, valid, safe = gather_rows(row_ids)
        scores = jnp.dot(rows, table_rows.T, preferred_element_type=jnp.float32) * inverse_root
        entity_coef = (jnp.exp(scores - total_rows[:, None]) - hits).astype(jnp.bfloat16)
        entity_grad = jnp.dot(entity_coef.T, rows, preferred_element_type=jnp.float32) * inverse_root
        returned = (jnp.dot(entity_coef, table_rows, preferred_element_type=jnp.float32) * inverse_root).astype(jnp.bfloat16)
        targets = jnp.where(valid, safe // PICKS, MENTIONS)
        carry = carry.at[targets].add(returned.astype(jnp.float32))
        new_first = BETA_ONE * first + (1.0 - BETA_ONE) * entity_grad
        new_second = BETA_TWO * second + (1.0 - BETA_TWO) * entity_grad * entity_grad
        new_rows = (table_rows.astype(jnp.float32) - STEP_SIZE * new_first / (jnp.sqrt(new_second) + EPSILON)).astype(jnp.bfloat16)
        return (carry, (new_rows, new_first, new_second))
    start = jnp.concatenate([direct_grad, jnp.zeros((1, D), jnp.float32)], axis=0)
    final, (new_entities, new_m, new_v) = lax.scan(update, start, (table, totals, entities, m_state, v_state))
    mention_grad = final[:MENTIONS]
    return (losses, mention_grad, centroid_grad, new_entities, new_m, new_v)
```

```python
import functools
import math

import jax
import jax.numpy as jnp
from jax import lax
from jax.experimental import pallas as pl
from jax.experimental.pallas import tpu as pltpu
from jax.sharding import PartitionSpec as P

BETA_ONE = 0.9
BETA_TWO = 0.999
STEP_SIZE = 0.05
EPSILON = 1e-08
MESH = pl.DeviceIdType.MESH
SLOTS = 16
MOST = 13
STRIDE = 45
F32 = jnp.float32
BF16 = jnp.bfloat16

NN = (((1,), (0,)), ((), ()))
NT = (((1,), (1,)), ((), ()))
TN = (((0,), (0,)), ((), ()))


def dot(a, b, dims=NN):
    return lax.dot_general(a, b, dims, preferred_element_type=F32)


def iota(shape, dim):
    return lax.broadcasted_iota(jnp.int32, shape, dim)


def kernel(
    n,
    n_gy,
    mentions_ref,
    centroids_ref,
    clusters_ref,
    gold_ref,
    map_ref,
    entities_ref,
    losses_ref,
    mention_grad_ref,
    centroid_grad_ref,
    entity_grad_ref,
    ent,
    snd,
    rcv,
    back,
    scores_ref,
    coef_ref,
    tags_ref,
    parts_ref,
    place_ref,
    gold_place_ref,
    norm_out,
    norm_in,
    total_out,
    total_in,
    ent_sem,
    row_ssem,
    row_rsem,
    norm_ssem,
    norm_rsem,
    total_ssem,
    total_rsem,
    back_ssem,
    back_rsem,
):
    count, width = mentions_ref.shape
    ents = entities_ref.shape[0]
    picks = clusters_ref.shape[1]
    group = 16
    chunks = n // group
    rows = group * SLOTS
    inverse_root = 1.0 / math.sqrt(width)
    gx = lax.axis_index("gx")
    gy = lax.axis_index("gy")
    me = gx * n_gy + gy
    gy_bits = n_gy.bit_length() - 1

    def partner(i):
        k = (i * STRIDE) & (n - 1)
        return (gx ^ lax.shift_right_logical(k, gy_bits), gy ^ (k & (n_gy - 1)))

    barrier = pltpu.get_barrier_semaphore()

    def greet(i, _):
        pl.semaphore_signal(barrier, inc=1, device_id=partner(i), device_id_type=MESH)
        return 0

    lax.fori_loop(1, n, greet, 0)
    ent_copy = pltpu.make_async_copy(entities_ref, ent, ent_sem)
    ent_copy.start()

    def send(src, dst, ssem, rsem, c, j):
        i = c * group + j

        def away():
            pltpu.make_async_remote_copy(
                src_ref=src.at[i],
                dst_ref=dst.at[i],
                send_sem=ssem,
                recv_sem=rsem,
                device_id=partner(i),
                device_id_type=MESH,
            ).start()

        if j == 0:
            pl.when(c > 0)(away)

            @pl.when(c == 0)
            def _():
                pltpu.make_async_copy(src.at[0], dst.at[0], rsem).start()
        else:
            away()

    def await_received(buf, c, sem):
        whole = buf.at[pl.ds(c * group, group)]
        pltpu.make_async_copy(whole, whole, sem).wait()

    def await_sent(buf, c, sem):
        @pl.when(c == 0)
        def _():
            part = buf.at[pl.ds(1, group - 1)]
            pltpu.make_async_copy(part, part, sem).wait()

        @pl.when(c > 0)
        def _():
            await_received(buf, c, sem)

    square = (n, n)
    named = jnp.zeros((count, n), F32)
    for j in range(picks):
        named = named + (clusters_ref[:, j : j + 1] == iota((count, n), 1)).astype(F32)
    gold_named = (clusters_ref[:, 0:1] == iota((count, n), 1)).astype(F32)
    steps = iota(square, 0)
    partners = me ^ ((steps * STRIDE) & (n - 1))
    owner = (partners == iota(square, 1)).astype(BF16)
    row_of = (map_ref[...] == iota(square, 0)).astype(BF16)
    step_of = dot(owner, row_of).astype(BF16)
    here = dot(step_of, named.astype(BF16), NT)
    gold_here = dot(step_of, gold_named.astype(BF16), NT)
    earlier = (iota((count, count), 0) < iota((count, count), 1)).astype(BF16)
    rank = dot(here.astype(BF16), earlier)
    place = jnp.where(here > 0.5, rank, -1.0)
    gold_place = jnp.where(gold_here > 0.5, rank, -1.0)
    place_ref[...] = place
    gold_place_ref[...] = gold_place

    lane = iota((count, 128), 1)
    eye = iota((count, count), 0) == iota((count, count), 1)

    def column(row):
        return jnp.sum(jnp.where(eye, row, 0.0), axis=1, keepdims=True)

    def as_row(col):
        return jnp.sum(jnp.where(eye, col, 0.0), axis=0, keepdims=True)

    def spread(places, parts):
        total = jnp.zeros((n, 128), F32)
        for r in range(MOST):
            values = jnp.zeros((count, 128), F32)
            for p, part in enumerate(parts):
                values = values + jnp.where(lane == 16 * p + r, part, 0.0)
            total = total + dot((places == float(r)).astype(BF16), values.astype(BF16))
        return total

    gold_tag = column((gold_ref[...] + 1).astype(F32))
    tag_high = jnp.floor(gold_tag * (1.0 / 64.0))
    tag_low = gold_tag - 64.0 * tag_high
    tag_rows = spread(gold_place, (tag_high, tag_low)).astype(BF16)
    norm_out[...] = tag_rows.astype(F32).reshape(n, 1, 128)

    sub3 = iota((group, SLOTS, 128), 1)
    lane3 = iota((group, SLOTS, 128), 2)

    def chosen(c):
        places = place_ref[pl.ds(c * group, group), :]
        picked = places[:, None, :] == iota((group, SLOTS, count), 1).astype(F32)
        return picked.astype(F32).reshape(rows, count).astype(BF16)

    put = iota((rows, group), 0) == iota((rows, group), 1) * SLOTS + MOST
    put = put.astype(F32).astype(BF16)

    pl.semaphore_wait(barrier, n - 1)

    def send_rows(c, _):
        block = dot(chosen(c), mentions_ref[...])
        tags = norm_out[pl.ds(c * group, group)].reshape(group, 128).astype(BF16)
        first = block[:, :128] + dot(put, tags)
        slab = snd.at[pl.ds(c * group, group)]
        slab[:, :, 0:128] = first.astype(BF16).reshape(group, SLOTS, 128)
        slab[:, :, 128:] = block[:, 128:].astype(BF16).reshape(group, SLOTS, width - 128)
        for j in range(group):
            send(snd, rcv, row_ssem.at[c], row_rsem.at[c], c, j)
        return 0

    lax.fori_loop(0, chunks, send_rows, 0)

    mentions = mentions_ref[...]
    centroids = centroids_ref[...]
    cluster_scores = dot(mentions, centroids, NT) * inverse_root
    top = jnp.max(cluster_scores, axis=1, keepdims=True)
    cluster_norm = jnp.log(jnp.sum(jnp.exp(cluster_scores - top), axis=1, keepdims=True)) + top
    cluster_gold = jnp.sum(cluster_scores * gold_named, axis=1, keepdims=True)
    cluster_coef = (jnp.exp(cluster_scores - cluster_norm) - gold_named).astype(BF16)
    mention_grad_ref[...] = dot(cluster_coef, centroids) * inverse_root
    shares = dot(cluster_coef, mentions, TN) * inverse_root
    high = shares.astype(BF16)
    low = (shares - high.astype(F32)).astype(BF16)
    parts_ref[0] = dot(owner, high).astype(BF16)
    parts_ref[1] = dot(owner, low).astype(BF16)
    cluster_loss = as_row(cluster_norm - cluster_gold)

    ent_copy.wait()

    tag_weight = jnp.where(lane3 == sub3, 64.0, 0.0) + jnp.where(lane3 == sub3 + 16, 1.0, 0.0)
    norm_lane = (lane3 == sub3).astype(F32)
    gold_lane = (lane3 == sub3 + 16).astype(F32)
    positions = (iota((rows, ents), 1) + 1).astype(F32)

    def score(c, _):
        await_received(rcv, c, row_rsem.at[c])
        block = rcv[pl.ds(c * group, group)]
        scores = dot(block.reshape(rows, width), ent[...], NT) * inverse_root
        tag_row = jnp.sum(
            jnp.where(sub3 == MOST, block[:, :, :128].astype(F32), 0.0), axis=1, keepdims=True
        )
        tags = jnp.sum(tag_row * tag_weight, axis=2, keepdims=True).reshape(rows, 1)
        scores_ref[pl.ds(c * rows, rows), :] = scores
        tags_ref[pl.ds(c * rows, rows), :] = tags
        most = jnp.max(scores, axis=1, keepdims=True)
        norm = jnp.log(jnp.sum(jnp.exp(scores - most), axis=1, keepdims=True)) + most
        gold = jnp.sum(jnp.where(positions == tags, scores, 0.0), axis=1, keepdims=True)
        message = jnp.sum(
            norm.reshape(group, SLOTS, 1) * norm_lane + gold.reshape(group, SLOTS, 1) * gold_lane,
            axis=1,
        )
        norm_out[pl.ds(c * group, group)] = message.reshape(group, 1, 128)
        for j in range(group):
            send(norm_out, norm_in, norm_ssem, norm_rsem, c, j)
        return 0

    lax.fori_loop(0, chunks, score, 0)

    pltpu.make_async_copy(norm_in, norm_in, norm_rsem).wait()
    received = norm_in[...].reshape(n, 128)
    norms = jnp.zeros((n, count), F32)
    golds = jnp.zeros((n, count), F32)
    place = place_ref[...]
    gold_place = gold_place_ref[...]
    for r in range(MOST):
        norms = jnp.where(place == float(r), received[:, r : r + 1], norms)
        golds = jnp.where(gold_place == float(r), received[:, 16 + r : 17 + r], golds)
    norms = jnp.where(place >= 0.0, norms, -1e30)
    most = jnp.max(norms, axis=0, keepdims=True)
    entity_norm = jnp.log(jnp.sum(jnp.exp(norms - most), axis=0, keepdims=True)) + most
    entity_gold = jnp.sum(golds, axis=0, keepdims=True)
    losses_ref[...] = cluster_loss + entity_norm - entity_gold
    total = column(entity_norm)
    total_high = total.astype(BF16).astype(F32)
    total_mid = (total - total_high).astype(BF16).astype(F32)
    total_low = total - total_high - total_mid
    total_out[...] = spread(place, (total_high, total_mid, total_low)).reshape(n, 1, 128)

    def send_totals(c, _):
        for j in range(group):
            send(total_out, total_in, total_ssem, total_rsem.at[c], c, j)
        return 0

    lax.fori_loop(0, chunks, send_totals, 0)

    total_weight = (
        (lane3 == sub3).astype(F32)
        + (lane3 == sub3 + 16).astype(F32)
        + (lane3 == sub3 + 32).astype(F32)
    )
    unused = iota((group, SLOTS, 1), 1) >= MOST
    put_high = put
    put_low = iota((rows, group), 0) == iota((rows, group), 1) * SLOTS + MOST + 1
    put_low = put_low.astype(F32).astype(BF16)

    def give_back(c, _):
        await_received(total_in, c, total_rsem.at[c])
        await_sent(snd, c, row_ssem.at[c])
        here = total_in[pl.ds(c * group, group)].reshape(group, 1, 128)
        totals = jnp.sum(here * total_weight, axis=2, keepdims=True)
        totals = jnp.where(unused, 1e30, totals).reshape(rows, 1)
        hits = (positions == tags_ref[pl.ds(c * rows, rows), :]).astype(F32)
        coef = (jnp.exp(scores_ref[pl.ds(c * rows, rows), :] - totals) - hits).astype(BF16)
        coef_ref[pl.ds(c * rows, rows), :] = coef
        returned = dot(coef, ent[...]) * inverse_root
        returned = returned + dot(put_high, parts_ref[0, pl.ds(c * group, group), :])
        returned = returned + dot(put_low, parts_ref[1, pl.ds(c * group, group), :])
        snd[pl.ds(c * group, group)] = returned.astype(BF16).reshape(group, SLOTS, width)
        for j in range(group):
            send(snd, back, back_ssem.at[c], back_rsem.at[c], c, j)
        return 0

    lax.fori_loop(0, chunks, give_back, 0)

    tile = 256

    def entity_grad(t, _):
        at = pl.ds(pl.multiple_of(t * tile, tile), tile)
        product = dot(coef_ref[:, at], rcv[...].reshape(n * SLOTS, width), TN)
        entity_grad_ref[at, :] = product * inverse_root
        return 0

    lax.fori_loop(0, ents // tile, entity_grad, 0)

    slot = iota((8, rows), 1) & (SLOTS - 1)
    carried = ((slot == MOST) | (slot == MOST + 1)).astype(F32).astype(BF16)
    centroid_grad_ref[...] = jnp.zeros_like(centroid_grad_ref)

    def collect(c, _):
        await_received(back, c, back_rsem.at[c])
        block = back[pl.ds(c * group, group)].reshape(rows, width)
        mention_grad_ref[...] += dot(chosen(c), block, TN)
        centroid_grad_ref[...] += dot(carried, block)
        return 0

    lax.fori_loop(0, chunks, collect, 0)

    def drain(c, _):
        await_sent(snd, c, back_ssem.at[c])
        return 0

    lax.fori_loop(0, chunks, drain, 0)
    for buf, sem in ((norm_out, norm_ssem), (total_out, total_ssem)):
        part = buf.at[pl.ds(1, n - 1)]
        pltpu.make_async_copy(part, part, sem).wait()


def body(n, n_gy, mentions, centroids, clusters, gold_entity, cluster_map, entities, m_state, v_state):
    count, width = mentions.shape
    ents = entities.shape[1]
    chunks = n // 16
    vmem = pl.BlockSpec(memory_space=pltpu.VMEM)
    dma = pltpu.SemaphoreType.DMA
    losses, mention_grad, centroid_grad, entity_grad = pl.pallas_call(
        functools.partial(kernel, n, n_gy),
        out_shape=(
            jax.ShapeDtypeStruct((1, count), F32),
            jax.ShapeDtypeStruct((count, width), F32),
            jax.ShapeDtypeStruct((8, width), F32),
            jax.ShapeDtypeStruct((ents, width), F32),
        ),
        in_specs=[vmem, vmem, vmem, vmem, vmem, pl.BlockSpec(memory_space=pl.ANY)],
        out_specs=(vmem, vmem, vmem, vmem),
        scratch_shapes=[
            pltpu.VMEM((ents, width), BF16),
            pltpu.VMEM((n, SLOTS, width), BF16),
            pltpu.VMEM((n, SLOTS, width), BF16),
            pltpu.VMEM((n, SLOTS, width), BF16),
            pltpu.VMEM((n * SLOTS, ents), F32),
            pltpu.VMEM((n * SLOTS, ents), BF16),
            pltpu.VMEM((n * SLOTS, 1), F32),
            pltpu.VMEM((2, n, width), BF16),
            pltpu.VMEM((n, count), F32),
            pltpu.VMEM((n, count), F32),
            pltpu.VMEM((n, 1, 128), F32),
            pltpu.VMEM((n, 1, 128), F32),
            pltpu.VMEM((n, 1, 128), F32),
            pltpu.VMEM((n, 1, 128), F32),
            dma,
            dma((chunks,)),
            dma((chunks,)),
            dma,
            dma,
            dma,
            dma((chunks,)),
            dma((chunks,)),
            dma((chunks,)),
        ],
        compiler_params=pltpu.CompilerParams(
            collective_id=0, has_side_effects=True, vmem_limit_bytes=52 << 20
        ),
        name="exchange",
    )(
        mentions,
        centroids,
        clusters,
        gold_entity.reshape(1, count),
        cluster_map.reshape(1, -1),
        entities.reshape(ents, width),
    )
    entity_grad = entity_grad.reshape(entities.shape)
    new_m = BETA_ONE * m_state + (1.0 - BETA_ONE) * entity_grad
    new_v = BETA_TWO * v_state + (1.0 - BETA_TWO) * entity_grad * entity_grad
    new_entities = (
        entities.astype(F32) - STEP_SIZE * new_m / (jnp.sqrt(new_v) + EPSILON)
    ).astype(BF16)
    return (
        losses.reshape(count),
        mention_grad,
        centroid_grad[:1],
        new_entities,
        new_m,
        new_v,
    )


def solution(mesh):
    both = ("gx", "gy")
    placed = (
        P(both, None),
        P(),
        P(both, None),
        P(both),
        P(),
        P(both, None, None),
        P(both, None, None),
        P(both, None, None),
    )
    n = mesh.shape["gx"] * mesh.shape["gy"]
    return jax.shard_map(
        functools.partial(body, n, mesh.shape["gy"]),
        mesh=mesh,
        in_specs=placed,
        out_specs=(
            P(both),
            P(both, None),
            P(both, None),
            P(both, None, None),
            P(both, None, None),
            P(both, None, None),
        ),
        check_vma=False,
    )
```

```python
import functools
import math

import jax
import jax.numpy as jnp
from jax import lax
from jax.experimental import pallas as pl
from jax.experimental.pallas import tpu as pltpu
from jax.sharding import PartitionSpec as P

BETA_ONE = 0.9
BETA_TWO = 0.999
STEP_SIZE = 0.05
EPSILON = 1e-08
MESH = pl.DeviceIdType.MESH
SLOTS = 16
MOST = 13
TILES = 7
SPARE = tuple((MOST + p % 3, p // 3) for p in range(MOST, 3 * TILES))
STRIDE = 45
F32 = jnp.float32
BF16 = jnp.bfloat16

NN = (((1,), (0,)), ((), ()))
NT = (((1,), (1,)), ((), ()))
TN = (((0,), (0,)), ((), ()))


def dot(a, b, dims=NN):
    return lax.dot_general(a, b, dims, preferred_element_type=F32)


def iota(shape, dim):
    return lax.broadcasted_iota(jnp.int32, shape, dim)


def kernel(
    n,
    n_gy,
    mentions_hbm,
    centroids_hbm,
    clusters_hbm,
    gold_hbm,
    map_hbm,
    entities_hbm,
    m_hbm,
    v_hbm,
    losses_ref,
    mention_grad_ref,
    centroid_grad_ref,
    new_entities_ref,
    new_m_ref,
    new_v_ref,
    mentions_ref,
    centroids_ref,
    clusters_ref,
    gold_ref,
    map_ref,
    ent,
    snd,
    rcv,
    back,
    rows_ref,
    scores_ref,
    coef_ref,
    tags_ref,
    tag_rows_ref,
    parts_ref,
    move_ref,
    unmove_ref,
    place_ref,
    gold_place_ref,
    norm_out,
    norm_in,
    total_out,
    total_in,
    in_sem,
    row_ssem,
    row_rsem,
    norm_ssem,
    norm_rsem,
    total_ssem,
    total_rsem,
    back_ssem,
    back_rsem,
):
    count, width = mentions_ref.shape
    ents = ent.shape[0]
    picks = clusters_ref.shape[0]
    kept = TILES * 128
    group = 16
    chunks = n // group
    rows = group * SLOTS
    inverse_root = 1.0 / math.sqrt(width)
    gx = lax.axis_index("gx")
    gy = lax.axis_index("gy")
    me = gx * n_gy + gy
    gy_bits = n_gy.bit_length() - 1

    def partner(i):
        k = (i * STRIDE) & (n - 1)
        return (gx ^ lax.shift_right_logical(k, gy_bits), gy ^ (k & (n_gy - 1)))

    copies = [
        pltpu.make_async_copy(src, dst, in_sem.at[at])
        for at, (src, dst) in enumerate(
            (
                (clusters_hbm, clusters_ref),
                (gold_hbm, gold_ref),
                (map_hbm, map_ref),
                (mentions_hbm, mentions_ref),
                (centroids_hbm, centroids_ref),
                (entities_hbm, ent),
                (m_hbm, new_m_ref),
                (v_hbm, new_v_ref),
            )
        )
    ]
    for copy in copies[:6]:
        copy.start()

    barrier = pltpu.get_barrier_semaphore()

    def greet(i, _):
        pl.semaphore_signal(barrier, inc=1, device_id=partner(i), device_id_type=MESH)
        return 0

    lax.fori_loop(1, n, greet, 0)

    def send(src, dst, ssem, rsem, c, j):
        i = c * group + j

        def away():
            pltpu.make_async_remote_copy(
                src_ref=src.at[i],
                dst_ref=dst.at[i],
                send_sem=ssem,
                recv_sem=rsem,
                device_id=partner(i),
                device_id_type=MESH,
            ).start()

        if j == 0:
            pl.when(c > 0)(away)

            @pl.when(c == 0)
            def _():
                pltpu.make_async_copy(src.at[0], dst.at[0], rsem).start()
        else:
            away()

    def await_received(buf, c, sem):
        whole = buf.at[pl.ds(c * group, group)]
        pltpu.make_async_copy(whole, whole, sem).wait()

    def await_sent(buf, c, sem):
        @pl.when(c == 0)
        def _():
            part = buf.at[pl.ds(1, group - 1)]
            pltpu.make_async_copy(part, part, sem).wait()

        @pl.when(c > 0)
        def _():
            await_received(buf, c, sem)

    for copy in copies[:3]:
        copy.wait()
    square = (n, n)
    named = jnp.zeros((n, count), F32)
    for j in range(picks):
        named = named + (clusters_ref[j : j + 1, :] == iota((n, count), 0)).astype(F32)
    gold_row = clusters_ref[0:1, :]
    gold_named = (gold_row == iota((n, count), 0)).astype(F32)
    steps = iota(square, 0)
    partners = me ^ ((steps * STRIDE) & (n - 1))
    owner = (partners == iota(square, 1)).astype(BF16)
    row_of = (map_ref[...] == iota(square, 0)).astype(BF16)
    step_of = dot(owner, row_of).astype(BF16)
    here = dot(step_of, named.astype(BF16))
    gold_here = dot(step_of, gold_named.astype(BF16))
    earlier = (iota((count, count), 0) < iota((count, count), 1)).astype(BF16)
    rank = dot(here.astype(BF16), earlier)
    place = jnp.where(here > 0.5, rank, -1.0)
    gold_place = jnp.where(gold_here > 0.5, rank, -1.0)
    place_ref[...] = place
    gold_place_ref[...] = gold_place

    lane = iota((count, 128), 1)
    eye = iota((count, count), 0) == iota((count, count), 1)

    def column(row):
        return jnp.sum(jnp.where(eye, row, 0.0), axis=1, keepdims=True)

    def as_row(col):
        return jnp.sum(jnp.where(eye, col, 0.0), axis=0, keepdims=True)

    def spread(places, parts):
        total = jnp.zeros((n, 128), F32)
        for r in range(MOST):
            values = jnp.zeros((count, 128), F32)
            for p, part in enumerate(parts):
                values = values + jnp.where(lane == 16 * p + r, part, 0.0)
            total = total + dot((places == float(r)).astype(BF16), values.astype(BF16))
        return total

    gold_tag = column((gold_ref[...] + 1).astype(F32))
    tag_high = jnp.floor(gold_tag * (1.0 / 64.0))
    tag_low = gold_tag - 64.0 * tag_high
    tag_rows_ref[...] = spread(gold_place, (tag_high, tag_low))

    sub3 = iota((group, SLOTS, 128), 1)
    lane3 = iota((group, SLOTS, 128), 2)

    def chosen(c):
        places = place_ref[pl.ds(c * group, group), :]
        picked = places[:, None, :] == iota((group, SLOTS, count), 1).astype(F32)
        return picked.astype(F32).reshape(rows, count).astype(BF16)

    to, come = iota((rows, rows), 0), iota((rows, rows), 1)
    for t in range((MOST + 2) // 3):
        for ref, a, b in ((move_ref, to, come), (unmove_ref, come, to)):
            same = (a - (a & (SLOTS - 1))) == (b - (b & (SLOTS - 1)))
            spare_row, row = a & (SLOTS - 1), b & (SLOTS - 1)
            fits = same & (spare_row >= MOST) & (row < MOST) & (row - 3 * t == spare_row - MOST)
            ref[t] = fits.astype(F32).astype(BF16)

    def pack(block, slab, spare):
        tail = block[:, kept:].astype(BF16)
        for t in range(TILES):
            part = block[:, t * 128 : (t + 1) * 128]
            if 3 * t < MOST:
                part = part + dot(move_ref[t], tail)
            part = part.reshape(group, SLOTS, 128)
            for (row, tile), values in zip(SPARE, spare, strict=True):
                if tile == t:
                    part = jnp.where(sub3 == row, values.astype(F32)[:, None, :], part)
            slab[:, :, t * 128 : (t + 1) * 128] = part.astype(BF16)

    def eighth(block):
        total = jnp.zeros((rows, 128), F32)
        for t in range((MOST + 2) // 3):
            total = total + dot(unmove_ref[t], block[:, t * 128 : (t + 1) * 128])
        return total.astype(BF16)

    def spare_row(block, p):
        row, tile = SPARE[p]
        part = block[:, :, tile * 128 : (tile + 1) * 128].astype(F32)
        return jnp.sum(jnp.where(sub3 == row, part, 0.0), axis=1)

    for copy in copies[3:5]:
        copy.wait()
    gold_hot = (column(gold_row.astype(F32)) == iota((count, n), 1).astype(F32)).astype(F32)
    mentions = mentions_ref[...]
    centroids = centroids_ref[...]
    cluster_scores = dot(mentions, centroids, NT) * inverse_root
    top = jnp.max(cluster_scores, axis=1, keepdims=True)
    cluster_norm = jnp.log(jnp.sum(jnp.exp(cluster_scores - top), axis=1, keepdims=True)) + top
    cluster_gold = jnp.sum(cluster_scores * gold_hot, axis=1, keepdims=True)
    cluster_coef = (jnp.exp(cluster_scores - cluster_norm) - gold_hot).astype(BF16)
    mention_grad_ref[...] = dot(cluster_coef, centroids) * inverse_root
    shares = dot(cluster_coef, mentions, TN) * inverse_root
    high = shares.astype(BF16)
    low = (shares - high.astype(F32)).astype(BF16)
    parts_ref[0] = dot(owner, high).astype(BF16)
    parts_ref[1] = dot(owner, low).astype(BF16)
    cluster_loss = as_row(cluster_norm - cluster_gold)
    centroid_grad_ref[...] = jnp.zeros_like(centroid_grad_ref)

    pl.semaphore_wait(barrier, n - 1)

    def send_rows(c, _):
        block = dot(chosen(c), mentions_ref[...])
        these = pl.ds(c * group, group)
        spare = [tag_rows_ref[these, :]]
        spare += [parts_ref[1, these, t * 128 : (t + 1) * 128] for t in range(TILES)]
        pack(block, snd.at[these], spare)
        for j in range(group):
            send(snd, rcv, row_ssem.at[c], row_rsem.at[c], c, j)
        return 0

    lax.fori_loop(0, chunks, send_rows, 0)
    for copy in copies[6:]:
        copy.start()
    copies[5].wait()

    tag_weight = jnp.where(lane3 == sub3, 64.0, 0.0) + jnp.where(lane3 == sub3 + 16, 1.0, 0.0)
    norm_lane = (lane3 == sub3).astype(F32)
    gold_lane = (lane3 == sub3 + 16).astype(F32)
    positions = (iota((rows, ents), 1) + 1).astype(F32)

    def score(c, _):
        await_received(rcv, c, row_rsem.at[c])
        block = rcv[pl.ds(c * group, group)]
        these = pl.ds(c * rows, rows)
        rows_ref[these, 0:kept] = block.reshape(rows, kept)
        rows_ref[these, kept:] = eighth(block.reshape(rows, kept))
        scores = dot(rows_ref[these, :], ent[...], NT) * inverse_root
        tag_row = spare_row(block, 0)[:, None, :]
        for t in range(TILES):
            at = slice(t * 128, (t + 1) * 128)
            centroid_grad_ref[:, at] += jnp.sum(spare_row(block, t + 1), axis=0, keepdims=True)
        tags = jnp.sum(tag_row * tag_weight, axis=2, keepdims=True).reshape(rows, 1)
        scores_ref[pl.ds(c * rows, rows), :] = scores
        tags_ref[pl.ds(c * rows, rows), :] = tags
        most = jnp.max(scores, axis=1, keepdims=True)
        norm = jnp.log(jnp.sum(jnp.exp(scores - most), axis=1, keepdims=True)) + most
        gold = jnp.sum(jnp.where(positions == tags, scores, 0.0), axis=1, keepdims=True)
        message = jnp.sum(
            norm.reshape(group, SLOTS, 1) * norm_lane + gold.reshape(group, SLOTS, 1) * gold_lane,
            axis=1,
        )
        norm_out[pl.ds(c * group, group), :, 0:128] = message.reshape(group, 1, 128)
        last = parts_ref[1, pl.ds(c * group, group), kept:].astype(F32)
        norm_out[pl.ds(c * group, group), :, 128:256] = last.reshape(group, 1, 128)
        for j in range(group):
            send(norm_out, norm_in, norm_ssem, norm_rsem, c, j)
        return 0

    lax.fori_loop(0, chunks, score, 0)

    pltpu.make_async_copy(norm_in, norm_in, norm_rsem).wait()
    received = norm_in[:, :, 0:128].reshape(n, 128)
    last = norm_in[:, :, 128:256].reshape(n, 128)
    centroid_grad_ref[:, kept:] += jnp.sum(last, axis=0, keepdims=True)
    norms = jnp.zeros((n, count), F32)
    golds = jnp.zeros((n, count), F32)
    place = place_ref[...]
    gold_place = gold_place_ref[...]
    for r in range(MOST):
        norms = jnp.where(place == float(r), received[:, r : r + 1], norms)
        golds = jnp.where(gold_place == float(r), received[:, 16 + r : 17 + r], golds)
    norms = jnp.where(place >= 0.0, norms, -1e30)
    most = jnp.max(norms, axis=0, keepdims=True)
    entity_norm = jnp.log(jnp.sum(jnp.exp(norms - most), axis=0, keepdims=True)) + most
    entity_gold = jnp.sum(golds, axis=0, keepdims=True)
    losses_ref[...] = cluster_loss + entity_norm - entity_gold
    total = column(entity_norm)
    total_high = total.astype(BF16).astype(F32)
    total_mid = (total - total_high).astype(BF16).astype(F32)
    total_low = total - total_high - total_mid
    total_out[...] = spread(place, (total_high, total_mid, total_low)).reshape(n, 1, 128)

    def send_totals(c, _):
        for j in range(group):
            send(total_out, total_in, total_ssem, total_rsem.at[c], c, j)
        return 0

    lax.fori_loop(0, chunks, send_totals, 0)

    total_weight = (
        (lane3 == sub3).astype(F32)
        + (lane3 == sub3 + 16).astype(F32)
        + (lane3 == sub3 + 32).astype(F32)
    )
    unused = iota((group, SLOTS, 1), 1) >= MOST
    def give_back(c, _):
        await_received(total_in, c, total_rsem.at[c])
        await_sent(snd, c, row_ssem.at[c])
        here = total_in[pl.ds(c * group, group)].reshape(group, 1, 128)
        totals = jnp.sum(here * total_weight, axis=2, keepdims=True)
        totals = jnp.where(unused, 1e30, totals).reshape(rows, 1)
        hits = (positions == tags_ref[pl.ds(c * rows, rows), :]).astype(F32)
        coef = (jnp.exp(scores_ref[pl.ds(c * rows, rows), :] - totals) - hits).astype(BF16)
        coef_ref[pl.ds(c * rows, rows), :] = coef
        returned = dot(coef, ent[...]) * inverse_root
        these = pl.ds(c * group, group)
        spare = [parts_ref[0, these, t * 128 : (t + 1) * 128] for t in range(TILES + 1)]
        pack(returned, snd.at[these], spare)
        for j in range(group):
            send(snd, back, back_ssem.at[c], back_rsem.at[c], c, j)
        return 0

    lax.fori_loop(0, chunks, give_back, 0)

    for copy in copies[6:]:
        copy.wait()
    tile = 256

    def step(t, _):
        at = pl.ds(pl.multiple_of(t * tile, tile), tile)
        grad = dot(coef_ref[:, at], rows_ref[...], TN) * inverse_root
        new_m = BETA_ONE * new_m_ref[at, :] + (1.0 - BETA_ONE) * grad
        new_v = BETA_TWO * new_v_ref[at, :] + (1.0 - BETA_TWO) * grad * grad
        new_m_ref[at, :] = new_m
        new_v_ref[at, :] = new_v
        moved = ent[at, :].astype(F32) - STEP_SIZE * new_m / (jnp.sqrt(new_v) + EPSILON)
        new_entities_ref[at, :] = moved.astype(BF16)
        return 0

    lax.fori_loop(0, ents // tile, step, 0)

    def collect(c, _):
        await_received(back, c, back_rsem.at[c])
        block = back[pl.ds(c * group, group)]
        flat = block.reshape(rows, kept)
        picked = chosen(c)
        mention_grad_ref[:, 0:kept] += dot(picked, flat, TN)
        mention_grad_ref[:, kept:] += dot(picked, eighth(flat), TN)
        for t in range(TILES + 1):
            at = slice(t * 128, (t + 1) * 128)
            centroid_grad_ref[:, at] += jnp.sum(spare_row(block, t), axis=0, keepdims=True)
        return 0

    lax.fori_loop(0, chunks, collect, 0)

    def drain(c, _):
        await_sent(snd, c, back_ssem.at[c])
        return 0

    lax.fori_loop(0, chunks, drain, 0)
    for buf, sem in ((norm_out, norm_ssem), (total_out, total_ssem)):
        part = buf.at[pl.ds(1, n - 1)]
        pltpu.make_async_copy(part, part, sem).wait()


def store(*refs):
    half = len(refs) // 2
    sems = refs[-1]
    copies = [
        pltpu.make_async_copy(src, dst, sems.at[at])
        for at, (src, dst) in enumerate(zip(refs[:half], refs[half:-1], strict=True))
    ]
    for copy in copies:
        copy.start()
    for copy in copies:
        copy.wait()


def body(n, n_gy, mentions, centroids, clusters, gold_entity, cluster_map, entities, m_state, v_state):
    count, width = mentions.shape
    picks = clusters.shape[1]
    ents = entities.shape[1]
    chunks = n // 16
    rows = 16 * SLOTS
    spread = (MOST + 2) // 3
    vmem = pl.BlockSpec(memory_space=pltpu.VMEM)
    anywhere = pl.BlockSpec(memory_space=pl.ANY)
    dma = pltpu.SemaphoreType.DMA
    results = (
        ((1, count), F32),
        ((count, width), F32),
        ((1, width), F32),
        ((ents, width), BF16),
        ((ents, width), F32),
        ((ents, width), F32),
    )
    held = pl.pallas_call(
        functools.partial(kernel, n, n_gy),
        out_shape=tuple(pltpu.VMEM(*result) for result in results),
        in_specs=[anywhere] * 8,
        out_specs=(vmem,) * 6,
        scratch_shapes=[
            pltpu.VMEM((count, width), BF16),
            pltpu.VMEM((n, width), BF16),
            pltpu.VMEM((picks, count), jnp.int32),
            pltpu.VMEM((1, count), jnp.int32),
            pltpu.VMEM((1, n), jnp.int32),
            pltpu.VMEM((ents, width), BF16),
            pltpu.VMEM((n, SLOTS, TILES * 128), BF16),
            pltpu.VMEM((n, SLOTS, TILES * 128), BF16),
            pltpu.VMEM((n, SLOTS, TILES * 128), BF16),
            pltpu.VMEM((n * SLOTS, width), BF16),
            pltpu.VMEM((n * SLOTS, ents), F32),
            pltpu.VMEM((n * SLOTS, ents), BF16),
            pltpu.VMEM((n * SLOTS, 1), F32),
            pltpu.VMEM((n, 128), F32),
            pltpu.VMEM((2, n, width), BF16),
            pltpu.VMEM((spread, rows, rows), BF16),
            pltpu.VMEM((spread, rows, rows), BF16),
            pltpu.VMEM((n, count), F32),
            pltpu.VMEM((n, count), F32),
            pltpu.VMEM((n, 1, 256), F32),
            pltpu.VMEM((n, 1, 256), F32),
            pltpu.VMEM((n, 1, 128), F32),
            pltpu.VMEM((n, 1, 128), F32),
            dma((8,)),
            dma((chunks,)),
            dma((chunks,)),
            dma,
            dma,
            dma,
            dma((chunks,)),
            dma((chunks,)),
            dma((chunks,)),
        ],
        compiler_params=pltpu.CompilerParams(
            collective_id=0, has_side_effects=True, vmem_limit_bytes=48 << 20
        ),
        name="exchange",
    )(
        mentions,
        centroids,
        clusters.T,
        gold_entity.reshape(1, count),
        cluster_map.reshape(1, -1),
        entities.reshape(ents, width),
        m_state.reshape(ents, width),
        v_state.reshape(ents, width),
    )
    losses, mention_grad, centroid_grad, new_entities, new_m, new_v = pl.pallas_call(
        store,
        out_shape=tuple(jax.ShapeDtypeStruct(*result) for result in results),
        in_specs=[vmem] * 6,
        out_specs=(anywhere,) * 6,
        scratch_shapes=[dma((6,))],
        compiler_params=pltpu.CompilerParams(vmem_limit_bytes=1 << 20),
        name="store",
    )(*(pltpu.with_memory_space_constraint(array, pltpu.VMEM) for array in held))
    return (
        losses.reshape(count),
        mention_grad,
        centroid_grad,
        new_entities.reshape(entities.shape),
        new_m.reshape(entities.shape),
        new_v.reshape(entities.shape),
    )


def solution(mesh):
    both = ("gx", "gy")
    placed = (
        P(both, None),
        P(),
        P(both, None),
        P(both),
        P(),
        P(both, None, None),
        P(both, None, None),
        P(both, None, None),
    )
    n = mesh.shape["gx"] * mesh.shape["gy"]
    return jax.shard_map(
        functools.partial(body, n, mesh.shape["gy"]),
        mesh=mesh,
        in_specs=placed,
        out_specs=(
            P(both),
            P(both, None),
            P(both, None),
            P(both, None, None),
            P(both, None, None),
            P(both, None, None),
        ),
        check_vma=False,
    )
```

```python
import functools
import math

import jax
import jax.numpy as jnp
import numpy as np
from jax import lax
from jax.experimental import pallas as pl
from jax.experimental.pallas import tpu as pltpu
from jax.sharding import PartitionSpec as P

BETA_ONE = 0.9
BETA_TWO = 0.999
STEP_SIZE = 0.05
EPSILON = 1e-08
MESH = pl.DeviceIdType.MESH
SLOTS = 16
MOST = 13
TILES = 7
SPARE = tuple((MOST + p % 3, p // 3) for p in range(MOST, 3 * TILES))
PAIRS = ((0, 10), (9, 12), (6, 3), (11, 4), (14, 1), (8, 2), (5, 15), (13, 7))
WORDS = tuple(
    int(np.array(sum(pair[p] << 4 * c for c, pair in enumerate(PAIRS)), np.uint32).astype(np.int32))
    for p in range(2)
)
F32 = jnp.float32
BF16 = jnp.bfloat16

NN = (((1,), (0,)), ((), ()))
NT = (((1,), (1,)), ((), ()))
TN = (((0,), (0,)), ((), ()))


def dot(a, b, dims=NN):
    return lax.dot_general(a, b, dims, preferred_element_type=F32)


def iota(shape, dim):
    return lax.broadcasted_iota(jnp.int32, shape, dim)


def kernel(
    n,
    n_gy,
    mentions_hbm,
    centroids_hbm,
    clusters_hbm,
    gold_hbm,
    map_hbm,
    entities_hbm,
    m_hbm,
    v_hbm,
    move_hbm,
    unmove_hbm,
    losses_ref,
    mention_grad_ref,
    centroid_grad_ref,
    new_entities_ref,
    new_m_ref,
    new_v_ref,
    mentions_ref,
    centroids_ref,
    clusters_ref,
    gold_ref,
    map_ref,
    ent,
    ent_t,
    snd,
    rcv,
    back,
    rows_ref,
    scores_ref,
    coef_ref,
    tags_ref,
    names_ref,
    tag_rows_ref,
    parts_ref,
    last_ref,
    move_ref,
    unmove_ref,
    place_ref,
    gold_place_ref,
    first_out,
    first_in,
    gold_out,
    gold_in,
    second_out,
    second_in,
    both_out,
    both_in,
    third_out,
    third_in,
    in_sem,
    row_ssem,
    row_rsem,
    step_ssem,
    step_rsem,
    third_rsem,
    back_ssem,
    back_rsem,
):
    count, width = mentions_ref.shape
    ents = ent.shape[0]
    picks = clusters_ref.shape[0]
    kept = TILES * 128
    group = 16
    chunks = n // group
    rows = group * SLOTS
    inverse_root = 1.0 / math.sqrt(width)
    gx = lax.axis_index("gx")
    gy = lax.axis_index("gy")
    me = gx * n_gy + gy
    gy_bits = n_gy.bit_length() - 1

    def other(c, j):
        a = lax.shift_right_logical(jnp.int32(WORDS[j & 1]), 4 * c) & (n // n_gy - 1)
        return a, ((j // 2 * 5) & (n_gy - 1)) ^ (3 * (j & 1))

    def partner(c, j):
        a, b = other(c, j)
        return gx ^ a, gy ^ b

    copies = [
        pltpu.make_async_copy(src, dst, in_sem.at[at])
        for at, (src, dst) in enumerate(
            (
                (clusters_hbm, clusters_ref),
                (gold_hbm, gold_ref),
                (map_hbm, map_ref),
                (mentions_hbm, mentions_ref),
                (centroids_hbm, centroids_ref),
                (entities_hbm, ent),
                (move_hbm, move_ref),
                (unmove_hbm, unmove_ref),
                (m_hbm, new_m_ref),
                (v_hbm, new_v_ref),
            )
        )
    ]
    for copy in copies[:8]:
        copy.start()

    barrier = pltpu.get_barrier_semaphore()

    def hops(k):
        codes = (k >> 5, (k >> 3) & 3, (k >> 1) & 3, k & 1)
        return sum((0, 1, 2, 1)[code] for code in codes)

    for k in sorted(range(1, n), key=hops, reverse=True):
        there = (gx ^ (k >> gy_bits), gy ^ (k & (n_gy - 1)))
        pl.semaphore_signal(barrier, inc=1, device_id=there, device_id_type=MESH)

    def send(src, dst, ssem, rsem, c, j):
        i = c * group + j

        def away():
            pltpu.make_async_remote_copy(
                src_ref=src.at[i],
                dst_ref=dst.at[i],
                send_sem=ssem,
                recv_sem=rsem,
                device_id=partner(c, j),
                device_id_type=MESH,
            ).start()

        if j == 0:
            pl.when(c > 0)(away)

            @pl.when(c == 0)
            def _():
                pltpu.make_async_copy(src.at[0], dst.at[0], rsem).start()
        else:
            away()

    def await_received(buf, c, sem):
        whole = buf.at[pl.ds(c * group, group)]
        pltpu.make_async_copy(whole, whole, sem).wait()

    def await_sent(buf, c, sem):
        @pl.when(c == 0)
        def _():
            part = buf.at[pl.ds(1, group - 1)]
            pltpu.make_async_copy(part, part, sem).wait()

        @pl.when(c > 0)
        def _():
            await_received(buf, c, sem)

    for copy in copies[:3]:
        copy.wait()
    square = (n, n)
    named = jnp.zeros((n, count), F32)
    for j in range(picks):
        named = named + (clusters_ref[j : j + 1, :] == iota((n, count), 0)).astype(F32)
    gold_row = clusters_ref[0:1, :]
    gold_named = (gold_row == iota((n, count), 0)).astype(F32)
    steps = iota(square, 0)
    turn = steps & 1
    a = jnp.where(turn == 0, WORDS[0], WORDS[1])
    a = lax.shift_right_logical(a, 4 * lax.shift_right_logical(steps, 4)) & (n // n_gy - 1)
    b = ((lax.shift_right_logical(steps & 15, 1) * 5) & (n_gy - 1)) ^ (3 * turn)
    partners = me ^ (a * n_gy + b)
    owner = (partners == iota(square, 1)).astype(BF16)
    row_of = (map_ref[...] == iota(square, 0)).astype(BF16)
    step_of = dot(owner, row_of).astype(BF16)
    here = dot(step_of, named.astype(BF16))
    gold_here = dot(step_of, gold_named.astype(BF16))
    earlier = (iota((count, count), 0) < iota((count, count), 1)).astype(BF16)
    rank = dot(here.astype(BF16), earlier)
    place = jnp.where(here > 0.5, rank, -1.0)
    gold_place = jnp.where(gold_here > 0.5, rank, -1.0)
    place_ref[...] = place
    gold_place_ref[...] = gold_place

    lane = iota((count, 128), 1)
    eye = iota((count, count), 0) == iota((count, count), 1)

    def column(row):
        return jnp.sum(jnp.where(eye, row, 0.0), axis=1, keepdims=True)

    def as_row(col):
        return jnp.sum(jnp.where(eye, col, 0.0), axis=0, keepdims=True)

    def spread(parts):
        total = jnp.zeros((n, 128), F32)
        for r in range(MOST):
            for places, values in parts:
                spot = jnp.zeros((count, 128), F32)
                for p, value in values:
                    spot = spot + jnp.where(lane == 16 * p + r, value, 0.0)
                total = total + dot((places == float(r)).astype(BF16), spot.astype(BF16))
        return total

    gold_tag = column((gold_ref[...] + 1).astype(F32))
    tag_high = jnp.floor(gold_tag * (1.0 / 64.0))
    tag_low = gold_tag - 64.0 * tag_high
    names = (iota((count, 1), 0) + 1).astype(F32)
    tag_rows_ref[...] = spread(
        ((gold_place, ((0, tag_high), (1, tag_low))), (place, ((2, names),)))
    )

    sub3 = iota((group, SLOTS, 128), 1)
    lane3 = iota((group, SLOTS, 128), 2)

    def chosen(c):
        places = place_ref[pl.ds(c * group, group), :]
        picked = places[:, None, :] == iota((group, SLOTS, count), 1).astype(F32)
        return picked.astype(F32).reshape(rows, count).astype(BF16)

    def pack(block, slab, spare):
        tail = block[:, kept:].astype(BF16)
        for t in range(TILES):
            part = block[:, t * 128 : (t + 1) * 128]
            if 3 * t < MOST:
                part = part + dot(move_ref[t], tail)
            part = part.reshape(group, SLOTS, 128)
            for (row, tile), values in zip(SPARE, spare, strict=True):
                if tile == t:
                    part = jnp.where(sub3 == row, values.astype(F32)[:, None, :], part)
            slab[:, :, t * 128 : (t + 1) * 128] = part.astype(BF16)

    def eighth(block):
        total = jnp.zeros((rows, 128), F32)
        for t in range((MOST + 2) // 3):
            total = total + dot(unmove_ref[t], block[:, t * 128 : (t + 1) * 128])
        return total.astype(BF16)

    def spare_row(block, p):
        row, tile = SPARE[p]
        part = block[:, :, tile * 128 : (tile + 1) * 128].astype(F32)
        return jnp.sum(jnp.where(sub3 == row, part, 0.0), axis=1)

    for copy in copies[3:5]:
        copy.wait()
    gold_hot = (column(gold_row.astype(F32)) == iota((count, n), 1).astype(F32)).astype(F32)
    mentions = mentions_ref[...]
    centroids = centroids_ref[...]
    cluster_scores = dot(mentions, centroids, NT) * inverse_root
    top = jnp.max(cluster_scores, axis=1, keepdims=True)
    cluster_norm = jnp.log(jnp.sum(jnp.exp(cluster_scores - top), axis=1, keepdims=True)) + top
    cluster_gold = jnp.sum(cluster_scores * gold_hot, axis=1, keepdims=True)
    cluster_coef = (jnp.exp(cluster_scores - cluster_norm) - gold_hot).astype(BF16)
    mention_grad_ref[...] = dot(cluster_coef, centroids) * inverse_root
    shares = dot(cluster_coef, mentions, TN) * inverse_root
    high = shares.astype(BF16)
    low = (shares - high.astype(F32)).astype(BF16)
    last_ref[...] = low[:, kept:].astype(F32)
    parts_ref[0] = dot(owner, high).astype(BF16)
    parts_ref[1] = dot(owner, low).astype(BF16)
    cluster_loss = as_row(cluster_norm - cluster_gold)
    centroid_grad_ref[...] = jnp.zeros_like(centroid_grad_ref)

    copies[6].wait()
    pl.semaphore_wait(barrier, n - 1)

    def send_rows(c, _):
        block = dot(chosen(c), mentions_ref[...])
        these = pl.ds(c * group, group)
        spare = [tag_rows_ref[these, :]]
        spare += [parts_ref[1, these, t * 128 : (t + 1) * 128] for t in range(TILES)]
        pack(block, snd.at[these], spare)
        for j in range(group):
            send(snd, rcv, row_ssem.at[c], row_rsem.at[c], c, j)
        return 0

    lax.fori_loop(0, chunks, send_rows, 0)
    for copy in copies[8:]:
        copy.start()
    copies[5].wait()
    copies[7].wait()
    ent_t[...] = ent[...].T

    tag_weight = jnp.where(lane3 == sub3, 64.0, 0.0) + jnp.where(lane3 == sub3 + 16, 1.0, 0.0)
    name_weight = (lane3 == sub3 + 32).astype(F32)
    lane_name = (lane3 + 1).astype(F32)
    def fill(q, _):
        a = lax.shift_right_logical(jnp.where((q & 1) == 0, WORDS[0], WORDS[1]), 4 * (q // 2))
        a = a & (n // n_gy - 1)
        gold_out[q, 1] = last_ref[pl.ds(pl.multiple_of((gx ^ a) * n_gy, n_gy), n_gy), :]
        return 0

    lax.fori_loop(0, n // n_gy, fill, 0)

    def along_gx(src, dst, ssem, rsem, c, turn):
        a, _ = other(c, turn)
        pltpu.make_async_remote_copy(
            src_ref=src,
            dst_ref=dst.at[2 * c + turn],
            send_sem=ssem,
            recv_sem=rsem,
            device_id=(gx ^ a, gy),
            device_id_type=MESH,
        ).start()

    positions = (iota((rows, ents), 1) + 1).astype(F32)

    def score(c, _):
        await_received(rcv, c, row_rsem.at[c])
        block = rcv[pl.ds(c * group, group)]
        these = pl.ds(c * rows, rows)
        rows_ref[these, 0:kept] = block.reshape(rows, kept)
        rows_ref[these, kept:] = eighth(block.reshape(rows, kept))
        scores = dot(rows_ref[these, :], ent_t[...]) * inverse_root
        tag_row = spare_row(block, 0)[:, None, :]
        for t in range(TILES):
            at = slice(t * 128, (t + 1) * 128)
            centroid_grad_ref[:, at] += jnp.sum(spare_row(block, t + 1), axis=0, keepdims=True)
        tags = jnp.sum(tag_row * tag_weight, axis=2, keepdims=True).reshape(rows, 1)
        scores_ref[pl.ds(c * rows, rows), :] = scores
        tags_ref[pl.ds(c * rows, rows), :] = tags
        names = jnp.sum(tag_row * name_weight, axis=2, keepdims=True)
        names_ref[pl.ds(c * rows, rows), :] = names.reshape(rows, 1)
        most = jnp.max(scores, axis=1, keepdims=True)
        norm = jnp.log(jnp.sum(jnp.exp(scores - most), axis=1, keepdims=True)) + most
        gold = jnp.sum(jnp.where(positions == tags, scores, 0.0), axis=1, keepdims=True)
        mine = names == lane_name
        norms = jnp.max(jnp.where(mine, norm.reshape(group, SLOTS, 1), -1e30), axis=1)
        golds = jnp.sum(jnp.where(mine, gold.reshape(group, SLOTS, 1), 0.0), axis=1)
        for j in range(group):
            at = pl.ds(other(c, j)[1] ^ gy, 1)
            first_out[2 * c + (j & 1), at, :] = norms[j : j + 1]
            gold_out[2 * c + (j & 1), 0, at, :] = golds[j : j + 1]

        for at, (src, dst) in enumerate(((first_out, first_in), (gold_out, gold_in))):

            @pl.when(c > 0)
            def _():
                along_gx(src.at[2 * c], dst, step_ssem.at[at], step_rsem.at[at], c, 0)

            along_gx(src.at[2 * c + 1], dst, step_ssem.at[at], step_rsem.at[at], c, 1)
        return 0

    lax.fori_loop(0, chunks, score, 0)

    def await_step(dst, at, sems):
        whole = dst.at[pl.ds(1, dst.shape[0] - 1)]
        pltpu.make_async_copy(whole, whole, sems.at[at]).wait()

    def combined(norms):
        most = functools.reduce(jnp.maximum, norms)
        return most + jnp.log(sum(jnp.exp(norm - most) for norm in norms))

    def along_gy(src, dst, at):
        for b in range(1, n_gy):
            pltpu.make_async_remote_copy(
                src_ref=src,
                dst_ref=dst.at[b],
                send_sem=step_ssem.at[at],
                recv_sem=step_rsem.at[at],
                device_id=(gx, gy ^ b),
                device_id_type=MESH,
            ).start()

    await_step(first_in, 0, step_rsem)
    second_out[...] = combined([first_out[0]] + [first_in[q] for q in range(1, n // n_gy)])
    along_gy(second_out, second_in, 2)
    await_step(second_in, 2, step_rsem)
    norm_tile = combined([second_out[...]] + [second_in[b] for b in range(1, n_gy)])
    third_out[...] = norm_tile
    for c in (*range(chunks - 2, chunks), *range(chunks - 2)):
        along_gx(third_out, third_in, step_ssem.at[4], third_rsem.at[c], c, 1)
        if c > 0:
            along_gx(third_out, third_in, step_ssem.at[4], third_rsem.at[c], c, 0)
        else:
            pltpu.make_async_copy(third_out, third_in.at[0], third_rsem.at[0]).start()
    own = iota((n_gy, count), 0) == gy

    def own_row(tile):
        return jnp.sum(jnp.where(own, tile, 0.0), axis=0, keepdims=True)

    losses_ref[...] = cluster_loss + own_row(norm_tile)

    unused = iota((group, SLOTS, 1), 1) >= MOST
    def give_back(t, _):
        c = lax.rem(t + chunks - 2, chunks)
        pair = third_in.at[pl.ds(2 * c, 2)]
        pltpu.make_async_copy(pair, pair, third_rsem.at[c]).wait()
        await_sent(snd, c, row_ssem.at[c])
        here = []
        for j in range(group):
            here.append(third_in[2 * c + (j & 1), pl.ds(other(c, j)[1] ^ gy, 1), :])
        here = jnp.concatenate(here, axis=0)[:, None, :]
        names = names_ref[pl.ds(c * rows, rows), :].reshape(group, SLOTS, 1)
        totals = jnp.sum(jnp.where(names == lane_name, here, 0.0), axis=2, keepdims=True)
        totals = jnp.where(unused, 1e30, totals).reshape(rows, 1)
        hits = (positions == tags_ref[pl.ds(c * rows, rows), :]).astype(F32)
        coef = (jnp.exp(scores_ref[pl.ds(c * rows, rows), :] - totals) - hits).astype(BF16)
        coef_ref[pl.ds(c * rows, rows), :] = coef
        returned = dot(coef, ent[...]) * inverse_root
        these = pl.ds(c * group, group)
        spare = [parts_ref[0, these, t * 128 : (t + 1) * 128] for t in range(TILES + 1)]
        pack(returned, snd.at[these], spare)
        for j in range(group):
            send(snd, back, back_ssem.at[c], back_rsem.at[c], c, j)
        return 0

    lax.fori_loop(0, chunks, give_back, 0)

    await_step(gold_in, 1, step_rsem)
    both_out[...] = sum((gold_in[q] for q in range(1, n // n_gy)), gold_out[0])
    along_gy(both_out, both_in, 3)

    for copy in copies[8:]:
        copy.wait()
    tile = 256

    def step(t, _):
        at = pl.ds(pl.multiple_of(t * tile, tile), tile)
        grad = dot(coef_ref[:, at], rows_ref[...], TN) * inverse_root
        new_m = BETA_ONE * new_m_ref[at, :] + (1.0 - BETA_ONE) * grad
        new_v = BETA_TWO * new_v_ref[at, :] + (1.0 - BETA_TWO) * grad * grad
        new_m_ref[at, :] = new_m
        new_v_ref[at, :] = new_v
        moved = ent[at, :].astype(F32) - STEP_SIZE * new_m / (jnp.sqrt(new_v) + EPSILON)
        new_entities_ref[at, :] = moved.astype(BF16)
        return 0

    lax.fori_loop(0, ents // tile, step, 0)

    def collect(t, _):
        c = lax.rem(t + chunks - 2, chunks)
        await_received(back, c, back_rsem.at[c])
        block = back[pl.ds(c * group, group)]
        flat = block.reshape(rows, kept)
        picked = chosen(c)
        mention_grad_ref[:, 0:kept] += dot(picked, flat, TN)
        mention_grad_ref[:, kept:] += dot(picked, eighth(flat), TN)
        for t in range(TILES + 1):
            at = slice(t * 128, (t + 1) * 128)
            centroid_grad_ref[:, at] += jnp.sum(spare_row(block, t), axis=0, keepdims=True)
        return 0

    lax.fori_loop(0, chunks, collect, 0)

    await_step(both_in, 3, step_rsem)
    both = sum((both_in[b] for b in range(1, n_gy)), both_out[...])
    losses_ref[...] -= own_row(both[0])
    centroid_grad_ref[:, kept:] += own_row(both[1])

    def drain(c, _):
        await_sent(snd, c, back_ssem.at[c])
        return 0

    lax.fori_loop(0, chunks, drain, 0)
    for at, dst in enumerate((first_in, gold_in, second_in, both_in, third_in)):
        await_step(dst, at, step_ssem)


def store(*refs):
    half = len(refs) // 2
    sems = refs[-1]
    pieces = []
    for src, dst in zip(refs[:half], refs[half:-1], strict=True):
        size = min(256, src.shape[0])
        for at in range(0, src.shape[0], size):
            pieces.append((src.at[pl.ds(at, size)], dst.at[pl.ds(at, size)]))
    copies = [
        pltpu.make_async_copy(src, dst, sems.at[at]) for at, (src, dst) in enumerate(pieces)
    ]
    for copy in copies:
        copy.start()
    for copy in copies:
        copy.wait()


def moves():
    spread = (MOST + 2) // 3
    move = np.zeros((spread, 16, SLOTS, 16, SLOTS), np.float32)
    for t in range(spread):
        for r in range(3 * t, min(3 * t + 3, MOST)):
            for block in range(16):
                move[t, block, MOST + r - 3 * t, block, r] = 1.0
    move = move.reshape(spread, 16 * SLOTS, 16 * SLOTS)
    return jnp.asarray(move, BF16), jnp.asarray(move.transpose(0, 2, 1), BF16)


def body(n, n_gy, mentions, centroids, clusters, gold_entity, cluster_map, entities, m_state, v_state):
    count, width = mentions.shape
    picks = clusters.shape[1]
    ents = entities.shape[1]
    chunks = n // 16
    rows = 16 * SLOTS
    spread = (MOST + 2) // 3
    vmem = pl.BlockSpec(memory_space=pltpu.VMEM)
    anywhere = pl.BlockSpec(memory_space=pl.ANY)
    dma = pltpu.SemaphoreType.DMA
    results = (
        ((1, count), F32),
        ((count, width), F32),
        ((1, width), F32),
        ((ents, width), BF16),
        ((ents, width), F32),
        ((ents, width), F32),
    )
    held = pl.pallas_call(
        functools.partial(kernel, n, n_gy),
        out_shape=tuple(pltpu.VMEM(*result) for result in results),
        in_specs=[anywhere] * 10,
        out_specs=(vmem,) * 6,
        scratch_shapes=[
            pltpu.VMEM((count, width), BF16),
            pltpu.VMEM((n, width), BF16),
            pltpu.VMEM((picks, count), jnp.int32),
            pltpu.VMEM((1, count), jnp.int32),
            pltpu.VMEM((1, n), jnp.int32),
            pltpu.VMEM((ents, width), BF16),
            pltpu.VMEM((width, ents), BF16),
            pltpu.VMEM((n, SLOTS, TILES * 128), BF16),
            pltpu.VMEM((n, SLOTS, TILES * 128), BF16),
            pltpu.VMEM((n, SLOTS, TILES * 128), BF16),
            pltpu.VMEM((n * SLOTS, width), BF16),
            pltpu.VMEM((n * SLOTS, ents), F32),
            pltpu.VMEM((n * SLOTS, ents), BF16),
            pltpu.VMEM((n * SLOTS, 1), F32),
            pltpu.VMEM((n * SLOTS, 1), F32),
            pltpu.VMEM((n, 128), F32),
            pltpu.VMEM((2, n, width), BF16),
            pltpu.VMEM((n, 128), F32),
            pltpu.VMEM((spread, rows, rows), BF16),
            pltpu.VMEM((spread, rows, rows), BF16),
            pltpu.VMEM((n, count), F32),
            pltpu.VMEM((n, count), F32),
            pltpu.VMEM((n // n_gy, n_gy, 128), F32),
            pltpu.VMEM((n // n_gy, n_gy, 128), F32),
            pltpu.VMEM((n // n_gy, 2, n_gy, 128), F32),
            pltpu.VMEM((n // n_gy, 2, n_gy, 128), F32),
            pltpu.VMEM((n_gy, 128), F32),
            pltpu.VMEM((n_gy, n_gy, 128), F32),
            pltpu.VMEM((2, n_gy, 128), F32),
            pltpu.VMEM((n_gy, 2, n_gy, 128), F32),
            pltpu.VMEM((n_gy, 128), F32),
            pltpu.VMEM((n // n_gy, n_gy, 128), F32),
            dma((10,)),
            dma((chunks,)),
            dma((chunks,)),
            dma((5,)),
            dma((4,)),
            dma((chunks,)),
            dma((chunks,)),
            dma((chunks,)),
        ],
        compiler_params=pltpu.CompilerParams(
            collective_id=0, has_side_effects=True, vmem_limit_bytes=48 << 20
        ),
        name="exchange",
    )(
        mentions,
        centroids,
        clusters.T,
        gold_entity.reshape(1, count),
        cluster_map.reshape(1, -1),
        entities.reshape(ents, width),
        m_state.reshape(ents, width),
        v_state.reshape(ents, width),
        *moves(),
    )
    losses, mention_grad, centroid_grad, new_entities, new_m, new_v = pl.pallas_call(
        store,
        out_shape=tuple(jax.ShapeDtypeStruct(*result) for result in results),
        in_specs=[vmem] * 6,
        out_specs=(anywhere,) * 6,
        scratch_shapes=[dma((15,))],
        compiler_params=pltpu.CompilerParams(vmem_limit_bytes=1 << 20),
        name="store",
    )(*(pltpu.with_memory_space_constraint(array, pltpu.VMEM) for array in held))
    return (
        losses.reshape(count),
        mention_grad,
        centroid_grad,
        new_entities.reshape(entities.shape),
        new_m.reshape(entities.shape),
        new_v.reshape(entities.shape),
    )


def solution(mesh):
    both = ("gx", "gy")
    placed = (
        P(both, None),
        P(),
        P(both, None),
        P(both),
        P(),
        P(both, None, None),
        P(both, None, None),
        P(both, None, None),
    )
    n = mesh.shape["gx"] * mesh.shape["gy"]
    return jax.shard_map(
        functools.partial(body, n, mesh.shape["gy"]),
        mesh=mesh,
        in_specs=placed,
        out_specs=(
            P(both),
            P(both, None),
            P(both, None),
            P(both, None, None),
            P(both, None, None),
            P(both, None, None),
        ),
        check_vma=False,
    )
```

```python
import functools
import math

import jax
import jax.numpy as jnp
import numpy as np
from jax import lax
from jax.experimental import pallas as pl
from jax.experimental.pallas import tpu as pltpu
from jax.sharding import PartitionSpec as P

BETA_ONE = 0.9
BETA_TWO = 0.999
STEP_SIZE = 0.05
EPSILON = 1e-08
MESH = pl.DeviceIdType.MESH
SLOTS = 16
MOST = 13
TILES = 7
SPARE = tuple((MOST + p % 3, p // 3) for p in range(MOST, 3 * TILES))
PAIRS = ((0, 10), (9, 12), (6, 3), (11, 4), (14, 1), (8, 2), (5, 15), (13, 7))
WORDS = tuple(
    int(np.array(sum(pair[p] << 4 * c for c, pair in enumerate(PAIRS)), np.uint32).astype(np.int32))
    for p in range(2)
)
F32 = jnp.float32
BF16 = jnp.bfloat16

NN = (((1,), (0,)), ((), ()))
NT = (((1,), (1,)), ((), ()))
TN = (((0,), (0,)), ((), ()))


def dot(a, b, dims=NN):
    return lax.dot_general(a, b, dims, preferred_element_type=F32)


def iota(shape, dim):
    return lax.broadcasted_iota(jnp.int32, shape, dim)


def kernel(
    n,
    n_gy,
    mentions_hbm,
    centroids_hbm,
    clusters_hbm,
    gold_hbm,
    map_hbm,
    entities_hbm,
    m_hbm,
    v_hbm,
    move_hbm,
    unmove_hbm,
    losses_ref,
    mention_grad_ref,
    centroid_grad_ref,
    new_entities_ref,
    new_m_ref,
    new_v_ref,
    mentions_ref,
    centroids_ref,
    clusters_ref,
    gold_ref,
    map_ref,
    ent,
    ent_t,
    snd,
    rcv,
    back,
    rows_ref,
    scores_ref,
    coef_ref,
    tags_ref,
    names_ref,
    tag_rows_ref,
    parts_ref,
    last_ref,
    move_ref,
    unmove_ref,
    place_ref,
    gold_place_ref,
    first_out,
    first_in,
    gold_out,
    gold_in,
    second_out,
    second_in,
    both_out,
    both_in,
    third_out,
    third_in,
    in_sem,
    row_ssem,
    row_rsem,
    step_ssem,
    step_rsem,
    third_rsem,
    back_ssem,
    back_rsem,
):
    count, width = mentions_ref.shape
    ents = ent.shape[0]
    picks = clusters_ref.shape[0]
    kept = TILES * 128
    group = 16
    chunks = n // group
    rows = group * SLOTS
    inverse_root = 1.0 / math.sqrt(width)
    gx = lax.axis_index("gx")
    gy = lax.axis_index("gy")
    me = gx * n_gy + gy
    gy_bits = n_gy.bit_length() - 1

    def other(c, j):
        a = lax.shift_right_logical(jnp.int32(WORDS[j & 1]), 4 * c) & (n // n_gy - 1)
        return a, ((j // 2 * 5) & (n_gy - 1)) ^ (3 * (j & 1))

    def partner(c, j):
        a, b = other(c, j)
        return gx ^ a, gy ^ b

    copies = [
        pltpu.make_async_copy(src, dst, in_sem.at[at])
        for at, (src, dst) in enumerate(
            (
                (clusters_hbm, clusters_ref),
                (gold_hbm, gold_ref),
                (map_hbm, map_ref),
                (mentions_hbm, mentions_ref),
                (centroids_hbm, centroids_ref),
                (entities_hbm, ent),
                (move_hbm, move_ref),
                (unmove_hbm, unmove_ref),
                (m_hbm, new_m_ref),
                (v_hbm, new_v_ref),
            )
        )
    ]
    for copy in copies[:8]:
        copy.start()

    barrier = pltpu.get_barrier_semaphore()

    def hops(k):
        codes = (k >> 5, (k >> 3) & 3, (k >> 1) & 3, k & 1)
        return sum((0, 1, 2, 1)[code] for code in codes)

    for k in sorted(range(1, n), key=hops, reverse=True):
        there = (gx ^ (k >> gy_bits), gy ^ (k & (n_gy - 1)))
        pl.semaphore_signal(barrier, inc=1, device_id=there, device_id_type=MESH)

    def send(src, dst, ssem, rsem, c, j):
        i = c * group + j

        def away():
            pltpu.make_async_remote_copy(
                src_ref=src.at[i],
                dst_ref=dst.at[i],
                send_sem=ssem,
                recv_sem=rsem,
                device_id=partner(c, j),
                device_id_type=MESH,
            ).start()

        if j == 0:
            pl.when(c > 0)(away)

            @pl.when(c == 0)
            def _():
                pltpu.make_async_copy(src.at[0], dst.at[0], rsem).start()
        else:
            away()

    def await_received(buf, c, sem):
        whole = buf.at[pl.ds(c * group, group)]
        pltpu.make_async_copy(whole, whole, sem).wait()

    def await_sent(buf, c, sem):
        @pl.when(c == 0)
        def _():
            part = buf.at[pl.ds(1, group - 1)]
            pltpu.make_async_copy(part, part, sem).wait()

        @pl.when(c > 0)
        def _():
            await_received(buf, c, sem)

    for copy in copies[:3]:
        copy.wait()
    square = (n, n)
    named = jnp.zeros((n, count), F32)
    for j in range(picks):
        named = named + (clusters_ref[j : j + 1, :] == iota((n, count), 0)).astype(F32)
    gold_row = clusters_ref[0:1, :]
    gold_named = (gold_row == iota((n, count), 0)).astype(F32)
    steps = iota(square, 0)
    turn = steps & 1
    a = jnp.where(turn == 0, WORDS[0], WORDS[1])
    a = lax.shift_right_logical(a, 4 * lax.shift_right_logical(steps, 4)) & (n // n_gy - 1)
    b = ((lax.shift_right_logical(steps & 15, 1) * 5) & (n_gy - 1)) ^ (3 * turn)
    partners = me ^ (a * n_gy + b)
    owner = (partners == iota(square, 1)).astype(BF16)
    row_of = (map_ref[...] == iota(square, 0)).astype(BF16)
    step_of = dot(owner, row_of).astype(BF16)
    here = dot(step_of, named.astype(BF16))
    gold_here = dot(step_of, gold_named.astype(BF16))
    earlier = (iota((count, count), 0) < iota((count, count), 1)).astype(BF16)
    rank = dot(here.astype(BF16), earlier)
    place = jnp.where(here > 0.5, rank, -1.0)
    gold_place = jnp.where(gold_here > 0.5, rank, -1.0)
    place_ref[...] = place
    gold_place_ref[...] = gold_place

    lane = iota((count, 128), 1)
    eye = iota((count, count), 0) == iota((count, count), 1)

    def column(row):
        return jnp.sum(jnp.where(eye, row, 0.0), axis=1, keepdims=True)

    def as_row(col):
        return jnp.sum(jnp.where(eye, col, 0.0), axis=0, keepdims=True)

    def spread(parts):
        total = jnp.zeros((n, 128), F32)
        for r in range(MOST):
            for places, values in parts:
                spot = jnp.zeros((count, 128), F32)
                for p, value in values:
                    spot = spot + jnp.where(lane == 16 * p + r, value, 0.0)
                total = total + dot((places == float(r)).astype(BF16), spot.astype(BF16))
        return total

    gold_tag = column((gold_ref[...] + 1).astype(F32))
    tag_high = jnp.floor(gold_tag * (1.0 / 64.0))
    tag_low = gold_tag - 64.0 * tag_high
    names = (iota((count, 1), 0) + 1).astype(F32)
    tag_rows_ref[...] = spread(
        ((gold_place, ((0, tag_high), (1, tag_low))), (place, ((2, names),)))
    )

    sub3 = iota((group, SLOTS, 128), 1)
    lane3 = iota((group, SLOTS, 128), 2)

    def chosen(c):
        places = place_ref[pl.ds(c * group, group), :]
        picked = places[:, None, :] == iota((group, SLOTS, count), 1).astype(F32)
        return picked.astype(F32).reshape(rows, count).astype(BF16)

    def pack(block, slab, spare):
        tail = block[:, kept:].astype(BF16)
        for t in range(TILES):
            part = block[:, t * 128 : (t + 1) * 128]
            if 3 * t < MOST:
                part = part + dot(move_ref[t], tail)
            part = part.reshape(group, SLOTS, 128)
            for (row, tile), values in zip(SPARE, spare, strict=True):
                if tile == t:
                    part = jnp.where(sub3 == row, values.astype(F32)[:, None, :], part)
            slab[:, :, t * 128 : (t + 1) * 128] = part.astype(BF16)

    def eighth(block):
        tiles = [block[:, t * 128 : (t + 1) * 128] for t in range((MOST + 2) // 3)]
        return dot(unmove_ref[...], jnp.concatenate(tiles, axis=0)).astype(BF16)

    def spare_row(block, p):
        row, tile = SPARE[p]
        part = block[:, :, tile * 128 : (tile + 1) * 128].astype(F32)
        return jnp.sum(jnp.where(sub3 == row, part, 0.0), axis=1)

    for copy in copies[3:5]:
        copy.wait()
    gold_hot = (column(gold_row.astype(F32)) == iota((count, n), 1).astype(F32)).astype(F32)
    mentions = mentions_ref[...]
    centroids = centroids_ref[...]
    cluster_scores = dot(mentions, centroids, NT) * inverse_root
    top = jnp.max(cluster_scores, axis=1, keepdims=True)
    cluster_norm = jnp.log(jnp.sum(jnp.exp(cluster_scores - top), axis=1, keepdims=True)) + top
    cluster_gold = jnp.sum(cluster_scores * gold_hot, axis=1, keepdims=True)
    cluster_coef = (jnp.exp(cluster_scores - cluster_norm) - gold_hot).astype(BF16)
    mention_grad_ref[...] = dot(cluster_coef, centroids) * inverse_root
    shares = dot(cluster_coef, mentions, TN) * inverse_root
    high = shares.astype(BF16)
    low = (shares - high.astype(F32)).astype(BF16)
    last_ref[...] = low[:, kept:].astype(F32)
    parts_ref[0] = dot(owner, high).astype(BF16)
    parts_ref[1] = dot(owner, low).astype(BF16)
    cluster_loss = as_row(cluster_norm - cluster_gold)
    centroid_grad_ref[...] = jnp.zeros_like(centroid_grad_ref)

    copies[6].wait()
    pl.semaphore_wait(barrier, n - 1)

    def send_rows(c, _):
        block = dot(chosen(c), mentions_ref[...])
        these = pl.ds(c * group, group)
        spare = [tag_rows_ref[these, :]]
        spare += [parts_ref[1, these, t * 128 : (t + 1) * 128] for t in range(TILES)]
        pack(block, snd.at[these], spare)
        for j in range(group):
            send(snd, rcv, row_ssem.at[c], row_rsem.at[c], c, j)
        return 0

    lax.fori_loop(0, chunks, send_rows, 0)
    for copy in copies[8:]:
        copy.start()
    copies[5].wait()
    copies[7].wait()
    ent_t[...] = ent[...].T

    tag_weight = jnp.where(lane3 == sub3, 64.0, 0.0) + jnp.where(lane3 == sub3 + 16, 1.0, 0.0)
    name_weight = (lane3 == sub3 + 32).astype(F32)
    lane_name = (lane3 + 1).astype(F32)
    def fill(q, _):
        a = lax.shift_right_logical(jnp.where((q & 1) == 0, WORDS[0], WORDS[1]), 4 * (q // 2))
        a = a & (n // n_gy - 1)
        gold_out[q, 1] = last_ref[pl.ds(pl.multiple_of((gx ^ a) * n_gy, n_gy), n_gy), :]
        return 0

    lax.fori_loop(0, n // n_gy, fill, 0)

    def along_gx(src, dst, ssem, rsem, c, turn):
        a, _ = other(c, turn)
        pltpu.make_async_remote_copy(
            src_ref=src,
            dst_ref=dst.at[2 * c + turn],
            send_sem=ssem,
            recv_sem=rsem,
            device_id=(gx ^ a, gy),
            device_id_type=MESH,
        ).start()

    positions = (iota((rows, ents), 1) + 1).astype(F32)

    def score(c, _):
        await_received(rcv, c, row_rsem.at[c])
        block = rcv[pl.ds(c * group, group)]
        these = pl.ds(c * rows, rows)
        rows_ref[these, 0:kept] = block.reshape(rows, kept)
        rows_ref[these, kept:] = eighth(block.reshape(rows, kept))
        scores = dot(rows_ref[these, :], ent_t[...]) * inverse_root
        tag_row = spare_row(block, 0)[:, None, :]
        for t in range(TILES):
            at = slice(t * 128, (t + 1) * 128)
            centroid_grad_ref[:, at] += jnp.sum(spare_row(block, t + 1), axis=0, keepdims=True)
        tags = jnp.sum(tag_row * tag_weight, axis=2, keepdims=True).reshape(rows, 1)
        scores_ref[pl.ds(c * rows, rows), :] = scores
        tags_ref[pl.ds(c * rows, rows), :] = tags
        names = jnp.sum(tag_row * name_weight, axis=2, keepdims=True)
        names_ref[pl.ds(c * rows, rows), :] = names.reshape(rows, 1)
        most = jnp.max(scores, axis=1, keepdims=True)
        norm = jnp.log(jnp.sum(jnp.exp(scores - most), axis=1, keepdims=True)) + most
        gold = jnp.sum(jnp.where(positions == tags, scores, 0.0), axis=1, keepdims=True)
        mine = names == lane_name
        norms = jnp.max(jnp.where(mine, norm.reshape(group, SLOTS, 1), -1e30), axis=1)
        golds = jnp.sum(jnp.where(mine, gold.reshape(group, SLOTS, 1), 0.0), axis=1)
        for j in range(group):
            at = pl.ds(other(c, j)[1] ^ gy, 1)
            first_out[2 * c + (j & 1), at, :] = norms[j : j + 1]
            gold_out[2 * c + (j & 1), 0, at, :] = golds[j : j + 1]

        for at, (src, dst) in enumerate(((first_out, first_in), (gold_out, gold_in))):

            @pl.when(c > 0)
            def _():
                along_gx(src.at[2 * c], dst, step_ssem.at[at], step_rsem.at[at], c, 0)

            along_gx(src.at[2 * c + 1], dst, step_ssem.at[at], step_rsem.at[at], c, 1)
        return 0

    lax.fori_loop(0, chunks, score, 0)

    def await_step(dst, at, sems):
        whole = dst.at[pl.ds(1, dst.shape[0] - 1)]
        pltpu.make_async_copy(whole, whole, sems.at[at]).wait()

    def combined(norms):
        most = functools.reduce(jnp.maximum, norms)
        return most + jnp.log(sum(jnp.exp(norm - most) for norm in norms))

    def along_gy(src, dst, at):
        for b in range(1, n_gy):
            pltpu.make_async_remote_copy(
                src_ref=src,
                dst_ref=dst.at[b],
                send_sem=step_ssem.at[at],
                recv_sem=step_rsem.at[at],
                device_id=(gx, gy ^ b),
                device_id_type=MESH,
            ).start()

    await_step(first_in, 0, step_rsem)
    second_out[...] = combined([first_out[0]] + [first_in[q] for q in range(1, n // n_gy)])
    along_gy(second_out, second_in, 2)
    await_step(second_in, 2, step_rsem)
    norm_tile = combined([second_out[...]] + [second_in[b] for b in range(1, n_gy)])
    third_out[...] = norm_tile
    for c in (chunks - 1, *range(chunks - 1)):
        along_gx(third_out, third_in, step_ssem.at[4], third_rsem.at[c], c, 1)
        if c > 0:
            along_gx(third_out, third_in, step_ssem.at[4], third_rsem.at[c], c, 0)
        else:
            pltpu.make_async_copy(third_out, third_in.at[0], third_rsem.at[0]).start()
    own = iota((n_gy, count), 0) == gy

    def own_row(tile):
        return jnp.sum(jnp.where(own, tile, 0.0), axis=0, keepdims=True)

    losses_ref[...] = cluster_loss + own_row(norm_tile)

    unused = iota((group, SLOTS, 1), 1) >= MOST
    def give_back(t, _):
        c = lax.rem(t + chunks - 1, chunks)
        pair = third_in.at[pl.ds(2 * c, 2)]
        pltpu.make_async_copy(pair, pair, third_rsem.at[c]).wait()
        await_sent(snd, c, row_ssem.at[c])
        here = []
        for j in range(group):
            here.append(third_in[2 * c + (j & 1), pl.ds(other(c, j)[1] ^ gy, 1), :])
        here = jnp.concatenate(here, axis=0)[:, None, :]
        names = names_ref[pl.ds(c * rows, rows), :].reshape(group, SLOTS, 1)
        totals = jnp.sum(jnp.where(names == lane_name, here, 0.0), axis=2, keepdims=True)
        totals = jnp.where(unused, 1e30, totals).reshape(rows, 1)
        hits = (positions == tags_ref[pl.ds(c * rows, rows), :]).astype(F32)
        coef = (jnp.exp(scores_ref[pl.ds(c * rows, rows), :] - totals) - hits).astype(BF16)
        coef_ref[pl.ds(c * rows, rows), :] = coef
        returned = dot(coef, ent[...]) * inverse_root
        these = pl.ds(c * group, group)
        spare = [parts_ref[0, these, t * 128 : (t + 1) * 128] for t in range(TILES + 1)]
        pack(returned, snd.at[these], spare)
        for j in range(group):
            send(snd, back, back_ssem.at[c], back_rsem.at[c], c, j)
        return 0

    lax.fori_loop(0, chunks, give_back, 0)

    await_step(gold_in, 1, step_rsem)
    both_out[...] = sum((gold_in[q] for q in range(1, n // n_gy)), gold_out[0])
    along_gy(both_out, both_in, 3)

    for copy in copies[8:]:
        copy.wait()
    tile = 256

    def step(t, _):
        at = pl.ds(pl.multiple_of(t * tile, tile), tile)
        grad = dot(coef_ref[:, at], rows_ref[...], TN) * inverse_root
        new_m = BETA_ONE * new_m_ref[at, :] + (1.0 - BETA_ONE) * grad
        new_v = BETA_TWO * new_v_ref[at, :] + (1.0 - BETA_TWO) * grad * grad
        new_m_ref[at, :] = new_m
        new_v_ref[at, :] = new_v
        moved = ent[at, :].astype(F32) - STEP_SIZE * new_m / (jnp.sqrt(new_v) + EPSILON)
        new_entities_ref[at, :] = moved.astype(BF16)
        return 0

    lax.fori_loop(0, ents // tile, step, 0)

    def collect(t, _):
        c = lax.rem(t + chunks - 1, chunks)
        await_received(back, c, back_rsem.at[c])
        block = back[pl.ds(c * group, group)]
        flat = block.reshape(rows, kept)
        picked = chosen(c)
        mention_grad_ref[:, 0:kept] += dot(picked, flat, TN)
        mention_grad_ref[:, kept:] += dot(picked, eighth(flat), TN)
        for t in range(TILES + 1):
            at = slice(t * 128, (t + 1) * 128)
            centroid_grad_ref[:, at] += jnp.sum(spare_row(block, t), axis=0, keepdims=True)
        return 0

    lax.fori_loop(0, chunks, collect, 0)

    await_step(both_in, 3, step_rsem)
    both = sum((both_in[b] for b in range(1, n_gy)), both_out[...])
    losses_ref[...] -= own_row(both[0])
    centroid_grad_ref[:, kept:] += own_row(both[1])

    def drain(c, _):
        await_sent(snd, c, back_ssem.at[c])
        return 0

    lax.fori_loop(0, chunks, drain, 0)
    for at, dst in enumerate((first_in, gold_in, second_in, both_in, third_in)):
        await_step(dst, at, step_ssem)


def store(*refs):
    half = len(refs) // 2
    sems = refs[-1]
    pieces = []
    for src, dst in zip(refs[:half], refs[half:-1], strict=True):
        size = min(256, src.shape[0])
        for at in range(0, src.shape[0], size):
            pieces.append((src.at[pl.ds(at, size)], dst.at[pl.ds(at, size)]))
    copies = [
        pltpu.make_async_copy(src, dst, sems.at[at]) for at, (src, dst) in enumerate(pieces)
    ]
    for copy in copies:
        copy.start()
    for copy in copies:
        copy.wait()


def moves():
    spread = (MOST + 2) // 3
    move = np.zeros((spread, 16, SLOTS, 16, SLOTS), np.float32)
    for t in range(spread):
        for r in range(3 * t, min(3 * t + 3, MOST)):
            for block in range(16):
                move[t, block, MOST + r - 3 * t, block, r] = 1.0
    move = move.reshape(spread, 16 * SLOTS, 16 * SLOTS)
    return jnp.asarray(move, BF16), jnp.asarray(move.transpose(2, 0, 1).reshape(16 * SLOTS, -1), BF16)


def body(n, n_gy, mentions, centroids, clusters, gold_entity, cluster_map, entities, m_state, v_state):
    count, width = mentions.shape
    picks = clusters.shape[1]
    ents = entities.shape[1]
    chunks = n // 16
    rows = 16 * SLOTS
    spread = (MOST + 2) // 3
    vmem = pl.BlockSpec(memory_space=pltpu.VMEM)
    anywhere = pl.BlockSpec(memory_space=pl.ANY)
    dma = pltpu.SemaphoreType.DMA
    results = (
        ((1, count), F32),
        ((count, width), F32),
        ((1, width), F32),
        ((ents, width), BF16),
        ((ents, width), F32),
        ((ents, width), F32),
    )
    held = pl.pallas_call(
        functools.partial(kernel, n, n_gy),
        out_shape=tuple(pltpu.VMEM(*result) for result in results),
        in_specs=[anywhere] * 10,
        out_specs=(vmem,) * 6,
        scratch_shapes=[
            pltpu.VMEM((count, width), BF16),
            pltpu.VMEM((n, width), BF16),
            pltpu.VMEM((picks, count), jnp.int32),
            pltpu.VMEM((1, count), jnp.int32),
            pltpu.VMEM((1, n), jnp.int32),
            pltpu.VMEM((ents, width), BF16),
            pltpu.VMEM((width, ents), BF16),
            pltpu.VMEM((n, SLOTS, TILES * 128), BF16),
            pltpu.VMEM((n, SLOTS, TILES * 128), BF16),
            pltpu.VMEM((n, SLOTS, TILES * 128), BF16),
            pltpu.VMEM((n * SLOTS, width), BF16),
            pltpu.VMEM((n * SLOTS, ents), F32),
            pltpu.VMEM((n * SLOTS, ents), BF16),
            pltpu.VMEM((n * SLOTS, 1), F32),
            pltpu.VMEM((n * SLOTS, 1), F32),
            pltpu.VMEM((n, 128), F32),
            pltpu.VMEM((2, n, width), BF16),
            pltpu.VMEM((n, 128), F32),
            pltpu.VMEM((spread, rows, rows), BF16),
            pltpu.VMEM((rows, spread * rows), BF16),
            pltpu.VMEM((n, count), F32),
            pltpu.VMEM((n, count), F32),
            pltpu.VMEM((n // n_gy, n_gy, 128), F32),
            pltpu.VMEM((n // n_gy, n_gy, 128), F32),
            pltpu.VMEM((n // n_gy, 2, n_gy, 128), F32),
            pltpu.VMEM((n // n_gy, 2, n_gy, 128), F32),
            pltpu.VMEM((n_gy, 128), F32),
            pltpu.VMEM((n_gy, n_gy, 128), F32),
            pltpu.VMEM((2, n_gy, 128), F32),
            pltpu.VMEM((n_gy, 2, n_gy, 128), F32),
            pltpu.VMEM((n_gy, 128), F32),
            pltpu.VMEM((n // n_gy, n_gy, 128), F32),
            dma((10,)),
            dma((chunks,)),
            dma((chunks,)),
            dma((5,)),
            dma((4,)),
            dma((chunks,)),
            dma((chunks,)),
            dma((chunks,)),
        ],
        compiler_params=pltpu.CompilerParams(
            collective_id=0, has_side_effects=True, vmem_limit_bytes=48 << 20
        ),
        name="exchange",
    )(
        mentions,
        centroids,
        clusters.T,
        gold_entity.reshape(1, count),
        cluster_map.reshape(1, -1),
        entities.reshape(ents, width),
        m_state.reshape(ents, width),
        v_state.reshape(ents, width),
        *moves(),
    )
    losses, mention_grad, centroid_grad, new_entities, new_m, new_v = pl.pallas_call(
        store,
        out_shape=tuple(jax.ShapeDtypeStruct(*result) for result in results),
        in_specs=[vmem] * 6,
        out_specs=(anywhere,) * 6,
        scratch_shapes=[dma((15,))],
        compiler_params=pltpu.CompilerParams(vmem_limit_bytes=1 << 20),
        name="store",
    )(*(pltpu.with_memory_space_constraint(array, pltpu.VMEM) for array in held))
    return (
        losses.reshape(count),
        mention_grad,
        centroid_grad,
        new_entities.reshape(entities.shape),
        new_m.reshape(entities.shape),
        new_v.reshape(entities.shape),
    )


def solution(mesh):
    both = ("gx", "gy")
    placed = (
        P(both, None),
        P(),
        P(both, None),
        P(both),
        P(),
        P(both, None, None),
        P(both, None, None),
        P(both, None, None),
    )
    n = mesh.shape["gx"] * mesh.shape["gy"]
    return jax.shard_map(
        functools.partial(body, n, mesh.shape["gy"]),
        mesh=mesh,
        in_specs=placed,
        out_specs=(
            P(both),
            P(both, None),
            P(both, None),
            P(both, None, None),
            P(both, None, None),
            P(both, None, None),
        ),
        check_vma=False,
    )
```
